512 devices in a mesh: group: 16 (over x, y), member: 32 (over z, core).
Axes of the slice: x: 4, y: 4, z: 16, core: 2. Of those that a mesh axis runs over, the one named last changes fastest.
Arguments:
- features: float32 [65536, 128], P(('group', 'member')), may hold values from -6 to 6
- w_self: float32 [128, 256], replicated, may hold values from -0.5 to 0.5
- w_neigh: float32 [128, 256], replicated, may hold values from -0.5 to 0.5
- bias: float32 [256], replicated, may hold values from -3 to 3
- cotangent: float32 [65536, 256], P(('group', 'member')), may hold values from -6 to 6
- edge_src: int32 [512, 1024], P(('group', 'member')), may hold values from 0 to 4607, as said below
- edge_dst: int32 [512, 1024], P(('group', 'member')), may hold values from 0 to 4095
- edge_count: int32 [512], P(('group', 'member')), may hold values from 768 to 1024, as said below
Outputs:
- hidden: float32 [65536, 256], P(('group', 'member'))
- feature_grad: float32 [65536, 128], P(('group', 'member'))
- grad_self: float32 [128, 256], replicated
- grad_neigh: float32 [128, 256], replicated
- grad_bias: float32 [256], replicated
The draws below stay inside these ranges and needn't reach their ends.
Inputs may be any that keep to these rules, and one draw needn't show every extreme that they name: `edge_src`: sources are drawn at random; about a quarter of the used slots name hubs. `edge_count`: some device uses all 1024 slots.
All inputs are finite; a program needn't handle non-finite values.
Results may differ from the reference program's by a relative error of at most 0.000073.
Values sent between devices are 32-bit elements; how exact they have to be, the bound alone decides.
A program may use at most 64 MiB of HBM per device.

```python
import jax
import jax.numpy as jnp
from jax import lax

IN = 128
HID = 256
V_DEV = 128
HUB_DEV = 1
EDGE_SLOTS = 1024
GROUP_ROWS = 4096
HUBS = 512
VERTS = 65536
N_MEMBER = 32
DEVICES = 512


def draw_edge_src(key, part):
    key = jax.random.fold_in(key, 11)
    key_pick, key_local, key_hub = jax.random.split(key, 3)
    pick = jax.random.randint(key_pick, (DEVICES, EDGE_SLOTS), 0, 4)
    local_src = jax.random.randint(key_local, (DEVICES, EDGE_SLOTS), 0, GROUP_ROWS)
    hub_src = jax.random.randint(key_hub, (DEVICES, EDGE_SLOTS), 0, HUBS) + GROUP_ROWS
    return jnp.where(pick == 0, hub_src, local_src).astype(jnp.int32)


def draw_edge_count(key, part):
    key = jax.random.fold_in(key, 23)
    key_count, key_full = jax.random.split(key)
    counts = jax.random.randint(key_count, (DEVICES,), 3 * EDGE_SLOTS // 4, EDGE_SLOTS + 1)
    full_device = jax.random.randint(key_full, (), 0, DEVICES)
    positions = jnp.arange(DEVICES, dtype=jnp.int32)
    return jnp.where(positions == full_device, EDGE_SLOTS, counts).astype(jnp.int32)


def set_ends(values, key, smallest, largest):
    index_at = [jax.random.randint(jax.random.fold_in(key, axis), (), 0, length) for axis, length in enumerate(values.shape)]
    longest = values.shape.index(max(values.shape))
    beside = index_at[:longest] + [(index_at[longest] + 1) % values.shape[longest]] + index_at[longest + 1:]
    return values.at[tuple(index_at)].set(smallest).at[tuple(beside)].set(largest)


def level_of(rng, extent, cuts, smallest, top_value):
    gain, own = 1.0, jax.random.fold_in(rng, 6)
    for axis_at, blocks in cuts:
        heights = jnp.exp(jax.random.uniform(jax.random.fold_in(own, axis_at), (blocks,), jnp.float32, smallest / len(cuts), top_value / len(cuts)))
        gain = gain * jnp.repeat(heights, extent[axis_at] // blocks).reshape([-1 if axis == axis_at else 1 for axis in range(len(extent))])
    return gain


def noise(stream_key, dims, spread, reach, shards=(), kind=jnp.bfloat16):
    level = level_of(stream_key, dims, shards, -0.22, 0.18) if shards else 1.0
    drawn = jax.random.normal(stream_key, dims, jnp.float32) * spread * level
    return jnp.minimum(jnp.maximum(drawn, -reach), reach).astype(kind)


def setup_inputs(seed: int = 0) -> dict:
    splits = jax.random.split(jax.random.key(seed), 9)
    features = noise(splits[0], (VERTS, IN), 1.0, 6.0, ((0, 512),), jnp.float32)
    w_self = noise(splits[1], (IN, HID), IN ** -0.5, 0.5, (), jnp.float32)
    w_neigh = noise(splits[2], (IN, HID), IN ** -0.5, 0.5, (), jnp.float32)
    bias = noise(splits[3], (HID,), 0.5, 3.0, (), jnp.float32)
    cotangent = noise(splits[4], (VERTS, HID), 1.0, 6.0, ((0, 512),), jnp.float32)
    edge_src = draw_edge_src(jax.random.fold_in(splits[8], 71), 0)
    edge_dst = set_ends(jax.random.randint(splits[6], (DEVICES, EDGE_SLOTS), 0, GROUP_ROWS), jax.random.fold_in(splits[6], 1), 0, GROUP_ROWS - 1).astype(jnp.int32)
    edge_count = draw_edge_count(jax.random.fold_in(splits[8], 71), 0)
    return {"features": features, "w_self": w_self, "w_neigh": w_neigh, "bias": bias, "cotangent": cotangent, "edge_src": edge_src, "edge_dst": edge_dst, "edge_count": edge_count}


def hub_vertex(hub_number):
    return hub_number // HUB_DEV * V_DEV + hub_number % HUB_DEV

def reference(features, w_self, w_neigh, bias, cotangent, edge_src, edge_dst, edge_count):
    highest = lax.Precision.HIGHEST
    verts = features.shape[0]
    device_ids = lax.broadcasted_iota(jnp.int32, (DEVICES, EDGE_SLOTS), 0)
    slot_ids = lax.broadcasted_iota(jnp.int32, (DEVICES, EDGE_SLOTS), 1)
    offset = device_ids // N_MEMBER * GROUP_ROWS
    from_hub = edge_src >= GROUP_ROWS
    hub_number = jnp.maximum(edge_src - GROUP_ROWS, 0)
    source = jnp.where(from_hub, hub_vertex(hub_number), offset + edge_src).reshape(-1).astype(jnp.int32)
    target = (offset + edge_dst).reshape(-1).astype(jnp.int32)
    in_use = (slot_ids < edge_count[:, None]).astype(jnp.float32).reshape(-1)
    gathered = jnp.take(features, source, axis=0) * in_use[:, None]
    summed = jax.ops.segment_sum(gathered, target, num_segments=verts)
    degree = jax.ops.segment_sum(in_use, target, num_segments=verts)
    divisor = jnp.maximum(degree, 1.0)
    neigh_mean = summed / divisor[:, None]
    pre_act = jnp.dot(features, w_self, precision=highest) + jnp.dot(neigh_mean, w_neigh, precision=highest) + bias
    sigmoid_z = jax.nn.sigmoid(pre_act)
    hidden = pre_act * sigmoid_z
    pre_grad = cotangent * sigmoid_z * (1.0 + pre_act * (1.0 - sigmoid_z))
    scale = 1.0 / jnp.sqrt(jnp.float32(verts))
    grad_self = jnp.dot(features.T, pre_grad, precision=highest) * scale
    grad_neigh = jnp.dot(neigh_mean.T, pre_grad, precision=highest) * scale
    grad_bias = lax.optimization_barrier(jnp.sum(pre_grad, axis=0)) * scale
    mean_grad = jnp.dot(pre_grad, w_neigh.T, precision=highest) / divisor[:, None]
    edge_values = jnp.take(mean_grad, target, axis=0) * in_use[:, None]
    from_edges = jax.ops.segment_sum(edge_values, source, num_segments=verts)
    feature_grad = jnp.dot(pre_grad, w_self.T, precision=highest) + from_edges
    return (hidden, feature_grad, grad_self, grad_neigh, grad_bias)
```

```python
import functools

import jax
import jax.numpy as jnp
from jax import lax
from jax.experimental import pallas as pl
from jax.experimental.pallas import tpu as pltpu
from jax.sharding import PartitionSpec as P

f32, bf16, i32 = jnp.float32, jnp.bfloat16, jnp.int32
MESH = pl.DeviceIdType.MESH
G, M = 16, 32
ROWS = 128
IN, HID = 128, 256
CHUNK = 1024
LOCAL = M * ROWS
LO = 256
HI_V = LOCAL // LO
HI_S = HI_V + G * M // LO
NT = (((1,), (1,)), ((), ()))


def dot(a, b, dims=(((1,), (0,)), ((), ()))):
    return lax.dot_general(a, b, dims, precision=lax.Precision.HIGHEST, preferred_element_type=f32)


def split8(x):
    high = x.astype(bf16).astype(f32)
    return jnp.concatenate([high, x - high], axis=0)


def fold8(x):
    return x + pltpu.roll(x, 4, 0)


def alternate(k, n):
    odd = lax.rem(k, 2)
    return odd * ((k + 1) // 2) + (1 - odd) * (n - k // 2)


def kernel(
    feat, w_self, w_neigh, bias, cot, e_src, e_dst, e_cnt,
    hid_o, fg_o, gs_o, gn_o, gb_o,
    oh_s, oh_d, r0, r1, v0, v1, acc, tab,
    hubrx, erx, fts, frx, hts, hrx, sums, sumrx, mgs, mgrx,
    g1s, g1rx, p2s, p2rx, p3s, p3rx, p4s, p4rx,
    bs, brx, hbs, hbrx, h2s, h2rx,
    ssem, rsem, esem,
):
    g, m = lax.axis_index("group"), lax.axis_index("member")
    core, z = lax.rem(m, 2), m // 2
    sib = m + 1 - 2 * core
    sub16 = lax.broadcasted_iota(i32, (16, 128), 0)
    iota16 = sub16.astype(f32).astype(bf16)
    pat16 = (sub16 // 8).astype(f32).astype(bf16)
    one16 = jnp.ones((16, 128), bf16)
    zero16 = jnp.zeros((16, 128), bf16)

    def copy_to(src, dst, k, gg, mm, recv=None):
        return pltpu.make_async_remote_copy(
            src_ref=src, dst_ref=dst, send_sem=ssem.at[k],
            recv_sem=rsem.at[k] if recv is None else recv,
            device_id=(gg, mm), device_id_type=MESH,
        )

    def over_members(src, dst, k, own=True):
        @pl.loop(1, M)
        def _(step):
            to = lax.rem(m + alternate(step, M), M)
            copy_to(src.at[to], dst.at[m], k, g, to).start()
        if own:
            dst[m] = src[m]

    def over_groups(src, dst, k):
        @pl.loop(1, G)
        def _(step):
            to = lax.rem(g + step, G)
            copy_to(src.at[to], dst.at[g], k, to, m).start()
        dst[g] = src[g]

    def wait(buf, n, sem):
        view = buf.at[pl.ds(0, n)]
        pltpu.make_async_copy(view, view, sem).wait()

    barrier = pltpu.get_barrier_semaphore()

    @pl.loop(1, M)
    def _(step):
        pl.semaphore_signal(barrier, inc=1, device_id=(g, lax.rem(m + step, M)), device_id_type=MESH)

    @pl.loop(1, G)
    def _(step):
        pl.semaphore_signal(barrier, inc=1, device_id=(lax.rem(g + step, G), m), device_id_type=MESH)

    def rows4(dst, x):
        for i in range(M):
            dst[i] = x[4 * i : 4 * i + 4, :]

    def joined(src):
        return jnp.concatenate([src[i] for i in range(M)], axis=0)

    with jax.named_scope("pack"):
        ft = feat[...].T
        rows4(fts, ft)
        src = e_src[...]
        hub = src - LOCAL
        src = jnp.where(hub >= 0, LOCAL + ((hub & (M - 1)) * G + (hub >> 5)), src)
        used = lax.broadcasted_iota(i32, (1, CHUNK), 1) < e_cnt[0]
        dst = jnp.where(used, e_dst[...], LOCAL)
        for r in range(8):
            erx[m, r : r + 1, :] = src[:, 128 * r : 128 * r + 128]
            erx[m, 8 + r : 9 + r, :] = dst[:, 128 * r : 128 * r + 128]

    pl.semaphore_wait(barrier, M - 1 + G - 1)

    hub_tile = feat.at[pl.ds(0, 8)]

    @pl.loop(1, G)
    def _(step):
        copy_to(hub_tile, hubrx.at[g], 0, lax.rem(g + step, G), m).start()

    hubrx[g] = feat[0:8, :]
    copy_to(erx.at[m], erx.at[m], 1, g, sib, esem.at[m]).start()

    @pl.loop(1, M // 2)
    def _(step):
        to = lax.rem(z + alternate(step, M // 2), M // 2) * 2 + core
        copy_to(erx.at[m], erx.at[m], 1, g, to, esem.at[m]).start()

    over_members(fts, frx, 2)

    wait(hubrx, G - 1, rsem.at[0])
    hub_rows = jnp.concatenate([hubrx[i][0:1, :] for i in range(G)] + [jnp.zeros((128 - G, 128), f32)], axis=0)
    rows4(hts, hub_rows.T)
    over_members(hts, hrx, 3)

    def one_hot(low, ref, slot):
        for r in range(8):
            row = jnp.broadcast_to(low[r : r + 1, :].astype(f32), (16, 128)).astype(bf16) - iota16
            for t in range(LO // 16):
                ref[slot, 16 * t : 16 * t + 16, 128 * r : 128 * r + 128] = jnp.where(
                    row == jnp.array(16 * t, bf16), one16, zero16
                )

    def both_hots(slot):
        one_hot(erx[slot, 0:8, :] & (LO - 1), oh_s, slot)
        one_hot(erx[slot, 8:16, :] & (LO - 1), oh_d, slot)

    def edge_wait(slot):
        pltpu.make_async_copy(erx.at[slot], erx.at[slot], esem.at[slot]).wait()

    both_hots(m)

    @pl.loop(1, M // 2)
    def _(step):
        slot = lax.rem(z + M // 2 - alternate(step, M // 2), M // 2) * 2 + core
        edge_wait(slot)
        copy_to(erx.at[slot], erx.at[slot], 1, g, sib, esem.at[slot]).start()
        both_hots(slot)

    edge_wait(sib)
    both_hots(sib)

    @pl.loop(1, M // 2)
    def _(step):
        slot = lax.rem(z + M // 2 - alternate(step, M // 2), M // 2) * 2 + 1 - core
        edge_wait(slot)
        both_hots(slot)

    def table(src):
        for t in range(HI_V // 2):
            for c in range(2):
                tab[16 * t : 16 * t + 16, 128 * c : 128 * c + 128] = jnp.concatenate(
                    [split8(src[4 * t + c]), split8(src[4 * t + 2 + c])], axis=0
                ).astype(bf16)

    def spread(values, high, v, n):
        w16 = jnp.concatenate([values, values], axis=0).astype(bf16)
        row = jnp.broadcast_to(high.astype(f32), (16, 128)).astype(bf16) - pat16
        for t in range(n // 2):
            v[16 * t : 16 * t + 16, :] = jnp.where(row == jnp.array(2 * t, bf16), w16, zero16)

    def aggregate(rows_in, n_in, n_out, forward, between):
        oh_in, oh_out = (oh_s, oh_d) if forward else (oh_d, oh_s)

        def gather(j, r):
            r[0:rows_in, :] = jnp.dot(tab[0:rows_in, :], oh_in[j], preferred_element_type=f32)

        def place(j, r, v):
            s_hi, d_hi = erx[j, 0:8, :] >> 8, erx[j, 8:16, :] >> 8
            in_hi, out_hi = (s_hi, d_hi) if forward else (d_hi, s_hi)
            for q in range(8):
                cols = pl.ds(128 * q, 128)
                high = jnp.broadcast_to(in_hi[q : q + 1, :], (8, 128))
                w = jnp.zeros((8, 128), f32)
                for h in range(n_in):
                    w = jnp.where(high == h, r[8 * h : 8 * h + 8, cols], w)
                spread(w, out_hi[q : q + 1, :], v.at[:, cols], n_out)
                if forward:
                    mine = jnp.broadcast_to(out_hi[q : q + 1, :], (16, 128)) == z
                    v[8 * n_out : 8 * n_out + 16, cols] = jnp.where(
                        mine & (sub16 == 0), jnp.float32(1), jnp.float32(0)
                    ).astype(bf16)

        def add(j, v):
            acc[...] += lax.dot_general(v[...], oh_out[j], NT, preferred_element_type=f32)

        acc[...] = jnp.zeros_like(acc)
        v1[...] = jnp.zeros_like(v1)
        gather(0, r0)

        def pair(i):
            j = 2 * i
            add(jnp.maximum(j - 1, 0), v1)
            place(j, r0, v0)
            gather(j + 1, r1)
            add(j, v0)
            place(j + 1, r1, v1)
            gather(jnp.minimum(j + 2, M - 1), r0)

        parts = len(between) + 1
        for part in range(parts):
            pl.loop(part * M // 2 // parts, (part + 1) * M // 2 // parts)(pair)
            if part < parts - 1:
                between[part]()
        add(M - 1, v1)

    def unpack(dst):
        for h in range(HI_V):
            for c in range(2):
                dst[2 * h + c] = fold8(acc[8 * h : 8 * h + 8, 128 * c : 128 * c + 128])[0:4, :]

    wait(frx, M - 1, rsem.at[2])
    with jax.named_scope("table"):
        table(frx)
    wait(hrx, M - 1, rsem.at[3])
    with jax.named_scope("hub_table"):
        for c in range(2):
            hubs = jnp.zeros((8, 128), f32)
            for k in range(8):
                both = jnp.concatenate([hrx[8 * c + k], hrx[16 + 8 * c + k]], axis=0)
                hubs = hubs + (pltpu.roll(both, 16 * k, 1) if k else both)
            tab[8 * HI_V : 8 * HI_S, 128 * c : 128 * c + 128] = jnp.concatenate(
                [split8(hubs[0:4, :]), split8(hubs[4:8, :])], axis=0
            ).astype(bf16)

    self_act = dot(feat[...], w_self[...]) + bias[...]
    with jax.named_scope("forward"):
        aggregate(8 * HI_S, HI_S, HI_V, True, [])
    with jax.named_scope("sums"):
        unpack(sums)
        over_members(sums, sumrx, 4)
        own = acc[8 * HI_V : 8 * HI_V + 1, :]
        degree = jnp.where(core == 0, own[:, 0:128], own[:, 128:256])
        inverse = 1.0 / jnp.maximum(degree, 1.0)
        wait(sumrx, M - 1, rsem.at[4])
    with jax.named_scope("dense"):
        mean_t = joined(sumrx) * inverse
        pre_act = self_act + dot(mean_t.T, w_neigh[...])
        sig = jax.nn.sigmoid(pre_act)
        hid_o[...] = pre_act * sig
        pre_grad = cot[...] * sig * (1.0 + pre_act * (1.0 - sig))
        rows4(mgs, dot(w_neigh[...], pre_grad, NT) * inverse)
        over_members(mgs, mgrx, 5)
        grad_s = dot(ft, pre_grad)
        grad_n = dot(mean_t, pre_grad)
        grad_b = jnp.broadcast_to(jnp.sum(pre_grad, axis=0, keepdims=True), (8, HID))
        for p in range(G):
            half = grad_s if p < G // 2 else grad_n
            at = 16 * (p % (G // 2))
            g1s[p, 0:16, :] = half[at : at + 16, :]
            g1s[p, 16:24, :] = grad_b
        over_groups(g1s, g1rx, 6)
        fg_o[...] = dot(pre_grad, w_self[...], NT)

    scale = 1.0 / (float(G * M * ROWS) ** 0.5)

    def reduce_groups():
        wait(g1rx, G - 1, rsem.at[6])
        total = g1rx[0]
        for i in range(1, G):
            total = total + g1rx[i]
        b0, b1 = total[16:17, 0:128], total[16:17, 128:256]
        rest = jnp.concatenate([b0, b1, jnp.zeros((1, 128), f32)], axis=0)
        for i in range(M):
            c = 128 * (i % 2)
            p2s[i] = jnp.concatenate([total[i // 2 : i // 2 + 1, c : c + 128], rest], axis=0)
        over_members(p2s, p2rx, 7)

    def reduce_members():
        wait(p2rx, M - 1, rsem.at[7])
        total = p2rx[0]
        for i in range(1, M):
            total = total + p2rx[i]
        total = total * scale
        gb_o[:, 0:128] = total[1:2, :]
        gb_o[:, 128:256] = total[2:3, :]
        p3s[...] = total

        @pl.loop(1, M)
        def _(step):
            to = lax.rem(m + alternate(step, M), M)
            copy_to(p3s, p3rx.at[m], 8, g, to).start()

        p3rx[m] = total

    def collect_members():
        wait(p3rx, M - 1, rsem.at[8])
        for i in range(M):
            c = 128 * (i % 2)
            p4s[i // 2 : i // 2 + 1, c : c + 128] = p3rx[i][0:1, :]

        @pl.loop(1, G)
        def _(step):
            copy_to(p4s, p4rx.at[g], 9, lax.rem(g + step, G), m).start()

        p4rx[g] = p4s[...]

    wait(mgrx, M - 1, rsem.at[5])
    with jax.named_scope("backward"):
        table(mgrx)
        aggregate(8 * HI_V, HI_V, HI_S, False, [reduce_groups, reduce_members, collect_members])
    with jax.named_scope("gradients"):
        for c in range(4):
            hubs = fold8(acc[8 * HI_V + 8 * (c // 2) : 8 * HI_V + 8 * (c // 2) + 8, 128 * (c % 2) : 128 * (c % 2) + 128])
            for k in range(8):
                hbs[8 * c + k] = (pltpu.roll(hubs, 128 - 16 * k, 1) if k else hubs)[0:4, :]
        over_members(hbs, hbrx, 10)
        unpack(bs)
        over_members(bs, brx, 11)
        wait(p4rx, G - 1, rsem.at[9])
        for p in range(G // 2):
            gs_o[16 * p : 16 * p + 16, :] = p4rx[p]
            gn_o[16 * p : 16 * p + 16, :] = p4rx[G // 2 + p]
        wait(hbrx, M - 1, rsem.at[10])
        hub_t = joined(hbrx).T
        for p in range(G):
            h2s[p] = jnp.broadcast_to(hub_t[p : p + 1, :], (8, 128))
        over_groups(h2s, h2rx, 12)
        wait(brx, M - 1, rsem.at[11])
        fg_o[...] += joined(brx).T
        wait(h2rx, G - 1, rsem.at[12])
        total = h2rx[0]
        for i in range(1, G):
            total = total + h2rx[i]
        first = lax.broadcasted_iota(i32, (8, 128), 0) == 0
        fg_o[0:8, :] += jnp.where(first, total, 0.0)

    wait(hubrx, G - 1, ssem.at[0])
    wait(erx, M - 1, ssem.at[1])
    wait(frx, M - 1, ssem.at[2])
    wait(hrx, M - 1, ssem.at[3])
    wait(sumrx, M - 1, ssem.at[4])
    wait(mgrx, M - 1, ssem.at[5])
    wait(g1rx, G - 1, ssem.at[6])
    wait(p2rx, M - 1, ssem.at[7])
    wait(p3rx, M - 1, ssem.at[8])
    wait(p4rx, G - 1, ssem.at[9])
    wait(hbrx, M - 1, ssem.at[10])
    wait(brx, M - 1, ssem.at[11])
    wait(h2rx, G - 1, ssem.at[12])


def on_device(features, w_self, w_neigh, bias, cotangent, edge_src, edge_dst, edge_count):
    vmem = pl.BlockSpec(memory_space=pltpu.VMEM)
    smem = pl.BlockSpec(memory_space=pltpu.SMEM)
    quads = pltpu.VMEM((M, 4, 128), f32)
    tiles = pltpu.VMEM((G, 8, 128), f32)
    scratch = [
        pltpu.VMEM((M, LO, CHUNK), bf16), pltpu.VMEM((M, LO, CHUNK), bf16),
        pltpu.VMEM((8 * HI_S, CHUNK), f32), pltpu.VMEM((8 * HI_S, CHUNK), f32),
        pltpu.VMEM((8 * HI_S, CHUNK), bf16), pltpu.VMEM((8 * HI_S, CHUNK), bf16),
        pltpu.VMEM((8 * HI_S, LO), f32), pltpu.VMEM((8 * HI_S, LO), bf16),
        tiles, pltpu.VMEM((M, 16, 128), i32), quads, quads, quads, quads, quads, quads, quads, quads,
        pltpu.VMEM((G, 24, HID), f32), pltpu.VMEM((G, 24, HID), f32), quads, quads,
        pltpu.VMEM((4, 128), f32), quads, pltpu.VMEM((16, HID), f32), pltpu.VMEM((G, 16, HID), f32),
        quads, quads, quads, quads, tiles, tiles,
        pltpu.SemaphoreType.DMA((13,)), pltpu.SemaphoreType.DMA((13,)), pltpu.SemaphoreType.DMA((M,)),
    ]
    hidden, feature_grad, grad_self, grad_neigh, grad_bias = pl.pallas_call(
        kernel,
        out_shape=(
            jax.ShapeDtypeStruct((ROWS, HID), f32),
            jax.ShapeDtypeStruct((ROWS, IN), f32),
            jax.ShapeDtypeStruct((IN, HID), f32),
            jax.ShapeDtypeStruct((IN, HID), f32),
            jax.ShapeDtypeStruct((1, HID), f32),
        ),
        in_specs=[vmem] * 7 + [smem],
        out_specs=[vmem] * 5,
        scratch_shapes=scratch,
        compiler_params=pltpu.CompilerParams(
            collective_id=0, has_side_effects=True, vmem_limit_bytes=56 << 20
        ),
        name="sage",
    )(features, w_self, w_neigh, bias.reshape(1, HID), cotangent, edge_src, edge_dst, edge_count)
    return hidden, feature_grad, grad_self, grad_neigh, grad_bias.reshape(HID)


def solution(mesh):
    rows = P(("group", "member"), None)
    return jax.shard_map(
        on_device,
        mesh=mesh,
        in_specs=(rows, P(), P(), P(), rows, rows, rows, P(("group", "member"))),
        out_specs=(rows, rows, P(), P(), P()),
        check_vma=False,
    )
```

```python
import jax
import jax.numpy as jnp
from jax import lax
from jax.experimental import pallas as pl
from jax.experimental.pallas import tpu as pltpu
from jax.sharding import PartitionSpec as P

f32, bf16, i32 = jnp.float32, jnp.bfloat16, jnp.int32
MESH = pl.DeviceIdType.MESH
G, M = 16, 32
ROWS = 128
IN, HID = 128, 256
CHUNK = 1024
LOCAL = M * ROWS
LO = 256
HI_V = LOCAL // LO
HI_S = HI_V + G * M // LO
N = 2
NT = (((1,), (1,)), ((), ()))


def dot(a, b, dims=(((1,), (0,)), ((), ()))):
    return lax.dot_general(a, b, dims, precision=lax.Precision.HIGHEST, preferred_element_type=f32)


def split8(x):
    high = x.astype(bf16).astype(f32)
    return jnp.concatenate([high, x - high], axis=0)


def fold8(x):
    return x + pltpu.roll(x, 4, 0)


def far_first(k, n):
    k = n - k
    odd = lax.rem(k, 2)
    return odd * ((k + 1) // 2) + (1 - odd) * (n - k // 2)


def lane_blocks():
    return lax.broadcasted_iota(i32, (8, 128), 1) >> 4, lax.broadcasted_iota(i32, (8, 128), 0)


def turned(x, rows):
    block, sub = lane_blocks()
    aligned = x
    for k in range(1, 8):
        aligned = jnp.where(sub == k, pltpu.roll(x, 16 * k, 1), aligned)
    out = []
    for c in range(rows):
        moved = pltpu.roll(aligned, 128 - 16 * c, 1) if c else aligned
        out.append(jnp.sum(jnp.where(block == sub, moved, 0.0), axis=0, keepdims=True))
    return out


def kernel(
    feat_h, w_self_h, w_neigh_h, bias_h, cot_h, src_h, dst_h, cnt_h,
    hid_o, fg_o, gs_o, gn_o, gb_o,
    feat, w_self, w_neigh, bias, cot, e_src, e_dst, e_cnt, hid, fg, gb,
    va, vb, acc, tab, hub_t,
    hubrx, erx, fts, frx, hts, hrx, sums, sumrx, mgs, mgrx,
    g1s, g1rx, p2s, p2rx, p3s, p3rx, p4s, p4rx,
    bs, brx, hbs, hbrx, h2s, h2rx,
    ssem, rsem, esem, isem, osem,
):
    g, m = lax.axis_index("group"), lax.axis_index("member")
    core, z = lax.rem(m, 2), m // 2
    sib = m + 1 - 2 * core
    sub16 = lax.broadcasted_iota(i32, (16, 128), 0)
    iota16 = sub16.astype(f32).astype(bf16)
    pat16 = (sub16 // 8).astype(f32).astype(bf16)
    one16 = jnp.ones((16, 128), bf16)
    zero16 = jnp.zeros((16, 128), bf16)

    barrier = pltpu.get_barrier_semaphore()

    @pl.loop(1, M)
    def _(step):
        to = lax.rem(m + far_first(step, M), M)
        pl.semaphore_signal(barrier, inc=1, device_id=(g, to), device_id_type=MESH)

    @pl.loop(1, G)
    def _(step):
        pl.semaphore_signal(barrier, inc=1, device_id=(lax.rem(g + step, G), m), device_id_type=MESH)

    fetches = [
        pltpu.make_async_copy(a, b, isem.at[k])
        for k, (a, b) in enumerate(
            [
                (feat_h, feat), (src_h, e_src), (dst_h, e_dst), (cnt_h, e_cnt),
                (w_self_h, w_self), (bias_h, bias), (w_neigh_h, w_neigh), (cot_h, cot),
            ]
        )
    ]
    for fetch in fetches:
        fetch.start()

    def copy_to(src, dst, k, gg, mm, recv=None):
        return pltpu.make_async_remote_copy(
            src_ref=src, dst_ref=dst, send_sem=ssem.at[k],
            recv_sem=rsem.at[k] if recv is None else recv,
            device_id=(gg, mm), device_id_type=MESH,
        )

    def over_members(src, dst, k):
        @pl.loop(1, M)
        def _(step):
            to = lax.rem(m + far_first(step, M), M)
            copy_to(src.at[to], dst.at[m], k, g, to).start()
        dst[m] = src[m]

    def over_groups(src, dst, k):
        @pl.loop(1, G)
        def _(step):
            to = lax.rem(g + step, G)
            copy_to(src.at[to], dst.at[g], k, to, m).start()
        dst[g] = src[g]

    def wait(buf, n, sem):
        view = buf.at[pl.ds(0, n)]
        pltpu.make_async_copy(view, view, sem).wait()

    def arrive(name, buf, n, k):
        with jax.named_scope(name):
            wait(buf, n, rsem.at[k])

    def rows4(dst, x):
        for i in range(M):
            dst[i] = x[4 * i : 4 * i + 4, :]

    def joined(src):
        return jnp.concatenate([src[i] for i in range(M)], axis=0)

    def stacked(src):
        return jnp.concatenate([src[i] for i in range(M)], axis=0)

    for k in range(4):
        fetches[k].wait()
    with jax.named_scope("pack"):
        ft = feat[...].T
        rows4(fts, ft)
        src = e_src[...]
        hub = src - LOCAL
        src = jnp.where(hub >= 0, LOCAL + ((hub & (M - 1)) * G + (hub >> 5)), src)
        used = lax.broadcasted_iota(i32, (1, CHUNK), 1) < e_cnt[...]
        dst = jnp.where(used, e_dst[...], LOCAL)
        for r in range(8):
            erx[m, r : r + 1, :] = src[:, 128 * r : 128 * r + 128]
            erx[m, 8 + r : 9 + r, :] = dst[:, 128 * r : 128 * r + 128]

    with jax.named_scope("entry_wait"):
        pl.semaphore_wait(barrier, M - 1 + G - 1)

    hub_tile = feat.at[pl.ds(0, 8)]

    @pl.loop(1, G)
    def _(step):
        copy_to(hub_tile, hubrx.at[g], 0, lax.rem(g + step, G), m).start()

    hubrx[g] = feat[0:8, :]
    copy_to(erx.at[m], erx.at[m], 1, g, sib, esem.at[m]).start()

    @pl.loop(1, M // 2)
    def _(step):
        to = lax.rem(z + far_first(step, M // 2), M // 2) * 2 + core
        copy_to(erx.at[m], erx.at[m], 1, g, to, esem.at[m]).start()

    over_members(fts, frx, 2)
    for k in range(4, 6):
        fetches[k].wait()
    self_act = dot(feat[...], w_self[...]) + bias[...]
    for k in range(6, 8):
        fetches[k].wait()

    arrive("hub_wait", hubrx, G - 1, 0)
    with jax.named_scope("hub_pack"):
        hub_rows = jnp.concatenate(
            [hubrx[i][0:1, :] for i in range(G)] + [jnp.zeros((128 - G, 128), f32)], axis=0
        )
        hub_t[...] = hub_rows.T
        packed = hub_t[pl.ds(0, M, stride=4), :]
        for c in range(1, 4):
            packed = packed + pltpu.roll(hub_t[pl.ds(c, M, stride=4), :], 16 * c, 1)
        for i in range(M):
            hts[i] = packed[i : i + 1, :]
        over_members(hts, hrx, 3)

    def edge_wait(slot):
        pltpu.make_async_copy(erx.at[slot], erx.at[slot], esem.at[slot]).wait()

    def nth_chip(step):
        return lax.rem(z + M // 2 - far_first(M // 2 - step, M // 2), M // 2) * 2

    with jax.named_scope("edges"):
        @pl.loop(1, M // 2)
        def _(step):
            slot = nth_chip(step) + core
            edge_wait(slot)
            copy_to(erx.at[slot], erx.at[slot], 1, g, sib, esem.at[slot]).start()

        edge_wait(sib)

        @pl.loop(1, M // 2)
        def _(step):
            edge_wait(nth_chip(step) + 1 - core)

    def table(src):
        for t in range(HI_V // 2):
            for c in range(2):
                tab[16 * t : 16 * t + 16, 128 * c : 128 * c + 128] = jnp.concatenate(
                    [split8(src[4 * t + c]), split8(src[4 * t + 2 + c])], axis=0
                ).astype(bf16)

    def spread_row(row, pattern):
        return jnp.broadcast_to(row.astype(f32), (16, 128)).astype(bf16) - pattern

    def hots(low, q):
        halves = []
        for r in (2 * q, 2 * q + 1):
            row = spread_row(low[r : r + 1, :], iota16)
            halves.append(
                jnp.concatenate(
                    [jnp.where(row == jnp.array(16 * t, bf16), one16, zero16) for t in range(LO // 16)], axis=0
                )
            )
        return jnp.concatenate(halves, axis=1)

    def aggregate(forward, between):
        n_in, n_out = (HI_S, HI_V) if forward else (HI_V, HI_S)
        i_at, o_at = (0, 8) if forward else (8, 0)

        def gather(j, v, k):
            ins, outs = erx[j, i_at : i_at + 8, :], erx[j, o_at : o_at + 8, :]
            in_lo, in_hi, out_hi = ins & (LO - 1), ins >> 8, outs >> 8
            for q in range(4):
                rows = jnp.dot(tab[0 : 8 * n_in, :], hots(in_lo, q), preferred_element_type=f32)
                for c in range(2):
                    r = 2 * q + c
                    cols = slice(128 * c, 128 * c + 128)
                    high = jnp.broadcast_to(in_hi[r : r + 1, :], (8, 128))
                    w = jnp.zeros((8, 128), f32)
                    for h in range(n_in):
                        w = jnp.where(high == h, rows[8 * h : 8 * h + 8, cols], w)
                    w16 = jnp.concatenate([w, w], axis=0).astype(bf16)
                    row = spread_row(out_hi[r : r + 1, :], pat16)
                    for t in range(n_out // 2):
                        v[4 * k + q, 16 * t : 16 * t + 16, cols] = jnp.where(
                            row == jnp.array(2 * t, bf16), w16, zero16
                        )
                    if forward:
                        mine = jnp.broadcast_to(out_hi[r : r + 1, :], (16, 128)) == z
                        v[4 * k + q, 8 * n_out : 8 * n_out + 16, cols] = jnp.where(
                            mine & (sub16 == 0), jnp.float32(1), jnp.float32(0)
                        ).astype(bf16)

        def scatter(j, v):
            total = None
            for k in range(N):
                out_lo = erx[j + k, o_at : o_at + 8, :] & (LO - 1)
                for q in range(4):
                    part = lax.dot_general(hots(out_lo, q), v[4 * k + q], NT, preferred_element_type=f32)
                    total = part if total is None else total + part
            acc[...] += total

        def step(i):
            j = 2 * N * i
            scatter(jnp.maximum(j - N, 0), vb)
            for k in range(N):
                gather(j + k, va, k)
            scatter(j, va)
            for k in range(N):
                gather(j + N + k, vb, k)

        acc[...] = jnp.zeros_like(acc)
        vb[...] = jnp.zeros_like(vb)
        steps, done = M // (2 * N), 0
        for until, action in between + [(steps, None)]:
            pl.loop(done, until)(step)
            done = until
            if action is not None:
                action()
        scatter(M - N, vb)
        last = jnp.concatenate([acc[:, 128:144], jnp.zeros((LO, 112), f32)], axis=1)
        return acc[:, 0:128].T, last.T[0:16, :]

    def unpack(dst, total):
        for h in range(HI_V):
            both = fold8(total[8 * h : 8 * h + 8, :])
            dst[2 * h] = both[0:4, 0:128]
            dst[2 * h + 1] = both[0:4, 128:256]

    arrive("feat_wait", frx, M - 1, 2)
    with jax.named_scope("table"):
        table(frx)
    arrive("hubcol_wait", hrx, M - 1, 3)
    with jax.named_scope("hub_table"):
        arrived = stacked(hrx)
        quarter = [jnp.concatenate(turned(arrived[8 * q : 8 * q + 8, :], 4), axis=0) for q in range(4)]
        for c in range(2):
            tab[8 * HI_V : 8 * HI_S, 128 * c : 128 * c + 128] = jnp.concatenate(
                [split8(quarter[c]), split8(quarter[2 + c])], axis=0
            ).astype(bf16)
    with jax.named_scope("forward"):
        total, own = aggregate(True, [])
    with jax.named_scope("sums"):
        unpack(sums, total)
        over_members(sums, sumrx, 4)
        degree = jnp.where(core == 0, own[0:1, 0:128], own[0:1, 128:256])
        inverse = 1.0 / jnp.maximum(degree, 1.0)
        arrive("sum_wait", sumrx, M - 1, 4)
    with jax.named_scope("dense"):
        mean_t = joined(sumrx) * inverse
        pre_act = self_act + dot(mean_t.T, w_neigh[...])
        sig = jax.nn.sigmoid(pre_act)
        pre_grad = cot[...] * sig * (1.0 + pre_act * (1.0 - sig))
        rows4(mgs, dot(w_neigh[...], pre_grad, NT) * inverse)
        over_members(mgs, mgrx, 5)
    with jax.named_scope("weight_grads"):
        hid[...] = pre_act * sig
        hid_out = pltpu.make_async_copy(hid, hid_o, osem.at[0])
        hid_out.start()
        grad_s = dot(ft, pre_grad)
        grad_n = dot(mean_t, pre_grad)
        grad_b = jnp.broadcast_to(jnp.sum(pre_grad, axis=0, keepdims=True), (8, HID))
        for p in range(G):
            half = grad_s if p < G // 2 else grad_n
            at = 16 * (p % (G // 2))
            g1s[p, 0:16, :] = half[at : at + 16, :]
            g1s[p, 16:24, :] = grad_b
        over_groups(g1s, g1rx, 6)
        fg[...] = dot(pre_grad, w_self[...], NT)

    scale = 1.0 / (float(G * M * ROWS) ** 0.5)

    def reduce_groups():
        arrive("p1_wait", g1rx, G - 1, 6)
        total = g1rx[0]
        for i in range(1, G):
            total = total + g1rx[i]
        b0, b1 = total[16:17, 0:128], total[16:17, 128:256]
        rest = jnp.concatenate([b0, b1, jnp.zeros((1, 128), f32)], axis=0)
        for i in range(M):
            c = 128 * (i % 2)
            p2s[i] = jnp.concatenate([total[i // 2 : i // 2 + 1, c : c + 128], rest], axis=0)
        over_members(p2s, p2rx, 7)

    def reduce_members():
        arrive("p2_wait", p2rx, M - 1, 7)
        total = p2rx[0]
        for i in range(1, M):
            total = total + p2rx[i]
        total = total * scale
        gb[:, 0:128] = total[1:2, :]
        gb[:, 128:256] = total[2:3, :]
        p3s[...] = total[0:1, :]

        @pl.loop(1, M)
        def _(step):
            copy_to(p3s, p3rx.at[m], 8, g, lax.rem(m + far_first(step, M), M)).start()

        p3rx[m] = p3s[...]

    def collect_members():
        arrive("p3_wait", p3rx, M - 1, 8)
        for i in range(M):
            c = 128 * (i % 2)
            p4s[i // 2 : i // 2 + 1, c : c + 128] = p3rx[i]

        @pl.loop(1, G)
        def _(step):
            copy_to(p4s, p4rx.at[g], 9, lax.rem(g + step, G), m).start()

        p4rx[g] = p4s[...]

    arrive("mean_wait", mgrx, M - 1, 5)
    with jax.named_scope("backward"):
        table(mgrx)
        total, hubs = aggregate(False, [(M // (16 * N), reduce_groups), (7 * M // (16 * N), reduce_members)])
    with jax.named_scope("tail"):
        for q in range(4):
            part = fold8(hubs[8 * (q // 2) : 8 * (q // 2) + 8, 128 * (q % 2) : 128 * (q % 2) + 128])
            for k, row in enumerate(turned(part, 8)):
                hbs[8 * q + k] = row
        over_members(hbs, hbrx, 10)
        unpack(bs, total)
        over_members(bs, brx, 11)
        collect_members()
        arrive("hubgrad_wait", hbrx, M - 1, 10)
        got = jnp.concatenate([stacked(hbrx), jnp.zeros((128 - M, 128), f32)], axis=0).T
        rows = got[0:16, :]
        for c in range(1, 4):
            rows = rows + pltpu.roll(got[16 * c : 16 * c + 16, :], 32 * c, 1)
        for p in range(G):
            h2s[p] = rows[p : p + 1, :]
        over_groups(h2s, h2rx, 12)
        arrive("grad_wait", brx, M - 1, 11)
        fg[...] += joined(brx).T
        arrive("p4_wait", p4rx, G - 1, 9)
        late = [
            pltpu.make_async_copy(p4rx.at[pl.ds(0, G // 2)], gs_o, osem.at[1]),
            pltpu.make_async_copy(p4rx.at[pl.ds(G // 2, G // 2)], gn_o, osem.at[2]),
            pltpu.make_async_copy(gb, gb_o, osem.at[3]),
        ]
        for copy in late:
            copy.start()
        arrive("hubsum_wait", h2rx, G - 1, 12)
        total = h2rx[0]
        for i in range(1, G):
            total = total + h2rx[i]
        lane = lax.broadcasted_iota(i32, (128, 128), 0)
        feature = lax.broadcasted_iota(i32, (128, 128), 1)
        order = jnp.where((lane & 31) * 4 + (lane >> 5) == feature, jnp.float32(1), jnp.float32(0))
        first = lax.broadcasted_iota(i32, (8, 128), 0) == 0
        total = jnp.where(first, jnp.broadcast_to(total, (8, 128)), 0.0)
        fg[0:8, :] += dot(total, order)
        fg_out = pltpu.make_async_copy(fg, fg_o, osem.at[4])
        fg_out.start()

    for buf, n, k in (
        (hubrx, G, 0), (erx, M, 1), (frx, M, 2), (hrx, M, 3), (sumrx, M, 4), (mgrx, M, 5), (g1rx, G, 6),
        (p2rx, M, 7), (p3rx, M, 8), (p4rx, G, 9), (hbrx, M, 10), (brx, M, 11), (h2rx, G, 12),
    ):
        wait(buf, n - 1, ssem.at[k])
    for copy in [hid_out] + late + [fg_out]:
        copy.wait()


def write_out(*refs):
    for a, b in zip(refs[:5], refs[5:]):
        b[...] = a[...]


def on_device(features, w_self, w_neigh, bias, cotangent, edge_src, edge_dst, edge_count):
    anywhere, vmem = pl.BlockSpec(memory_space=pl.ANY), pl.BlockSpec(memory_space=pltpu.VMEM)
    quads = pltpu.VMEM((M, 4, 128), f32)
    lines = pltpu.VMEM((M, 1, 128), f32)
    args = [features, w_self, w_neigh, bias.reshape(1, HID), cotangent, edge_src, edge_dst, edge_count.reshape(1, 1)]
    scratch = [pltpu.VMEM(a.shape, a.dtype) for a in args] + [
        pltpu.VMEM((ROWS, HID), f32), pltpu.VMEM((ROWS, IN), f32), pltpu.VMEM((1, HID), f32),
        pltpu.VMEM((4 * N, 8 * HI_S, 256), bf16), pltpu.VMEM((4 * N, 8 * HI_S, 256), bf16),
        pltpu.VMEM((LO, 8 * HI_S), f32), pltpu.VMEM((8 * HI_S, LO), bf16), pltpu.VMEM((128, 128), f32),
        pltpu.VMEM((G, 8, 128), f32), pltpu.VMEM((M, 16, 128), i32),
        quads, quads, lines, lines, quads, quads, quads, quads,
        pltpu.VMEM((G, 24, HID), f32), pltpu.VMEM((G, 24, HID), f32), quads, quads,
        pltpu.VMEM((1, 128), f32), lines, pltpu.VMEM((16, HID), f32), pltpu.VMEM((G, 16, HID), f32),
        quads, quads, lines, lines, pltpu.VMEM((G, 1, 128), f32), pltpu.VMEM((G, 1, 128), f32),
        pltpu.SemaphoreType.DMA((13,)), pltpu.SemaphoreType.DMA((13,)), pltpu.SemaphoreType.DMA((M,)),
        pltpu.SemaphoreType.DMA((8,)), pltpu.SemaphoreType.DMA((5,)),
    ]
    shapes = [(ROWS, HID), (ROWS, IN), (G // 2, 16, HID), (G // 2, 16, HID), (1, HID)]
    results = pl.pallas_call(
        kernel,
        out_shape=[jax.ShapeDtypeStruct(s, f32) for s in shapes],
        in_specs=[anywhere] * 8,
        out_specs=[anywhere] * 5,
        scratch_shapes=scratch,
        compiler_params=pltpu.CompilerParams(
            collective_id=0, has_side_effects=True, vmem_limit_bytes=56 << 20
        ),
        name="sage",
    )(*args)
    final = [(ROWS, HID), (ROWS, IN), (IN, HID), (IN, HID), (1, HID)]
    results = pl.pallas_call(
        write_out,
        out_shape=[jax.ShapeDtypeStruct(s, f32) for s in final],
        in_specs=[vmem] * 5,
        out_specs=[vmem] * 5,
        name="write_out",
    )(*[r.reshape(s) for r, s in zip(results, final)])
    return (*results[:4], results[4].reshape(HID))


def solution(mesh):
    rows = P(("group", "member"), None)
    return jax.shard_map(
        on_device,
        mesh=mesh,
        in_specs=(rows, P(), P(), P(), rows, rows, rows, P(("group", "member"))),
        out_specs=(rows, rows, P(), P(), P()),
        check_vma=False,
    )
```

```python
import jax
import jax.numpy as jnp
from jax import lax
from jax.experimental import pallas as pl
from jax.experimental.pallas import tpu as pltpu
from jax.sharding import PartitionSpec as P

f32, bf16, i32 = jnp.float32, jnp.bfloat16, jnp.int32
MESH = pl.DeviceIdType.MESH
G, M = 16, 32
ROWS = 128
IN, HID = 128, 256
CHUNK = 1024
LOCAL = M * ROWS
LO = 256
HI_V = LOCAL // LO
HI_H = G * M // LO
N = 4
NT = (((1,), (1,)), ((), ()))


def halves(x):
    high = x.astype(bf16)
    return high, (x - high.astype(f32)).astype(bf16)


def dot(a, b, dims=(((1,), (0,)), ((), ()))):
    (a0, a1), (b0, b1) = halves(a), halves(b)

    def part(x, y):
        return lax.dot_general(x, y, dims, preferred_element_type=f32)

    return part(a0, b0) + (part(a0, b1) + part(a1, b0))


def split8(x):
    high = x.astype(bf16).astype(f32)
    return jnp.concatenate([high, x - high], axis=0)


def fold8(x):
    return x + pltpu.roll(x, 4, 0)


def each_far_first(me, n, send):
    send(lax.rem(me + n // 2, n))

    @pl.loop(1, n // 2)
    def _(near):
        send(lax.rem(me + n // 2 + near, n))
        send(lax.rem(me + n // 2 - near, n))


def kernel(
    feat_h, w_self_h, w_neigh_h, bias_h, cot_h, src_h, dst_h, cnt_h,
    hid_o, fg_o, gs_o, gn_o, gb_o,
    feat, w_self, w_neigh, bias, cot, e_src, e_dst, e_cnt, hid, fg, gb,
    va, vb, acc, tab, own,
    hubs, hub_rows, erx, fts, frx, sums, sumrx, mgs, mgrx,
    g1s, g1rx, p2s, p2rx, p3s, p3rx, p4s, p4rx,
    bs, brx, hgs, hgrx, h2s, h2rx,
    ssem, rsem, esem, isem, osem,
):
    g, m = lax.axis_index("group"), lax.axis_index("member")
    core, z = lax.rem(m, 2), m // 2
    sib = m + 1 - 2 * core
    sub16 = lax.broadcasted_iota(i32, (16, 128), 0)
    iota16 = sub16.astype(f32).astype(bf16)
    pat16 = (sub16 // 8).astype(f32).astype(bf16)
    one16 = jnp.ones((16, 128), bf16)
    zero16 = jnp.zeros((16, 128), bf16)

    barrier = pltpu.get_barrier_semaphore()
    with jax.named_scope("greet"):

        def greet(to):
            pl.semaphore_signal(barrier, inc=1, device_id=(g, to), device_id_type=MESH)

        each_far_first(m, M, greet)

        @pl.loop(1, G)
        def _(step):
            pl.semaphore_signal(barrier, inc=1, device_id=(lax.rem(g + step, G), m), device_id_type=MESH)

    fetches = [
        pltpu.make_async_copy(a, b, isem.at[k])
        for k, (a, b) in enumerate(
            [
                (feat_h, feat), (src_h, e_src), (dst_h, e_dst), (cnt_h, e_cnt),
                (w_self_h, w_self), (bias_h, bias), (w_neigh_h, w_neigh), (cot_h, cot),
            ]
        )
    ]
    for fetch in fetches:
        fetch.start()

    def copy_to(src, dst, k, gg, mm, recv=None):
        return pltpu.make_async_remote_copy(
            src_ref=src, dst_ref=dst, send_sem=ssem.at[k],
            recv_sem=rsem.at[k] if recv is None else recv,
            device_id=(gg, mm), device_id_type=MESH,
        )

    def over_members(src, dst, k):
        each_far_first(m, M, lambda to: copy_to(src.at[to], dst.at[m], k, g, to).start())
        dst[m] = src[m]

    def to_members(src, dst, k):
        each_far_first(m, M, lambda to: copy_to(src, dst.at[m], k, g, to).start())

    def over_groups(src, dst, k):
        @pl.loop(1, G)
        def _(step):
            to = lax.rem(g + step, G)
            copy_to(src.at[to], dst.at[g], k, to, m).start()
        dst[g] = src[g]

    def wait(buf, n, sem):
        view = buf.at[pl.ds(0, n)]
        pltpu.make_async_copy(view, view, sem).wait()

    def arrive(name, buf, n, k):
        with jax.named_scope(name):
            wait(buf, n, rsem.at[k])

    def rows4(dst, x):
        for i in range(M):
            dst[i] = x[4 * i : 4 * i + 4, :]

    def joined(src):
        return jnp.concatenate([src[i] for i in range(M)], axis=0)

    for k in range(4):
        fetches[k].wait()
    with jax.named_scope("pack"):
        ft = feat[...].T
        rows4(fts, ft)
        src = e_src[...]
        used = lax.broadcasted_iota(i32, (1, CHUNK), 1) < e_cnt[...]
        dst = jnp.where(used, e_dst[...], LOCAL)
        for r in range(8):
            erx[m, r : r + 1, :] = src[:, 128 * r : 128 * r + 128]
            erx[m, 8 + r : 9 + r, :] = dst[:, 128 * r : 128 * r + 128]

    with jax.named_scope("entry_wait"):
        pl.semaphore_wait(barrier, M - 1 + G - 1)

    hubs[m] = feat[0:1, :]
    to_members(hubs.at[m], hubs, 0)
    over_members(fts, frx, 2)

    def edge_wait(slot):
        pltpu.make_async_copy(erx.at[slot], erx.at[slot], esem.at[slot]).wait()

    def edge_send(slot, to):
        copy_to(erx.at[slot], erx.at[slot], 1, g, to, esem.at[slot]).start()

    edge_send(m, sib)

    def nth_slot(n, other):
        odd = lax.rem(n, 2)
        ahead = odd * ((n + 1) // 2) + (1 - odd) * (M // 2 - n // 2)
        return lax.rem(z + ahead, M // 2) * 2 + (1 - core if other else core)

    @pl.loop(1, M // 2)
    def _(n):
        edge_send(m, nth_slot(n, False))

    def hand_on(quarter):
        @pl.loop(0, 4)
        def _(k):
            slot = nth_slot(4 * quarter + k, False)
            edge_wait(slot)
            edge_send(slot, sib)

    def others(quarter):
        @pl.loop(0, 4)
        def _(k):
            edge_wait(nth_slot(4 * quarter + k, True))

    with jax.named_scope("edges_first"):
        @pl.loop(1, 4)
        def _(k):
            slot = nth_slot(k, False)
            edge_wait(slot)
            edge_send(slot, sib)

    def table(src):
        for t in range(HI_V // 2):
            for c in range(2):
                tab[16 * t : 16 * t + 16, 128 * c : 128 * c + 128] = jnp.concatenate(
                    [split8(src[4 * t + c]), split8(src[4 * t + 2 + c])], axis=0
                ).astype(bf16)

    def spread_row(row, pattern):
        return jnp.broadcast_to(row.astype(f32), (16, 128)).astype(bf16) - pattern

    def hots(low, q):
        halves = []
        for r in (2 * q, 2 * q + 1):
            row = spread_row(low[r : r + 1, :], iota16)
            halves.append(
                jnp.concatenate(
                    [jnp.where(row == jnp.array(16 * t, bf16), one16, zero16) for t in range(LO // 16)], axis=0
                )
            )
        return jnp.concatenate(halves, axis=1)

    def aggregate(forward, between):
        i_at, o_at = (0, 8) if forward else (8, 0)
        width = 8 * HI_V + (16 if forward else 0)

        def slot(c, k):
            return nth_slot(c // 2 + k // 2, k % 2 == 1)

        def gather(j, v, k):
            j = slot(j, k)
            ins, outs = erx[j, i_at : i_at + 8, :], erx[j, o_at : o_at + 8, :]
            in_lo, in_hi, out_hi = ins & (LO - 1), ins >> 8, outs >> 8
            for q in range(4):
                rows = jnp.dot(tab[...], hots(in_lo, q), preferred_element_type=f32)
                for c in range(2):
                    r = 2 * q + c
                    cols = slice(128 * c, 128 * c + 128)
                    high = jnp.broadcast_to(in_hi[r : r + 1, :], (8, 128))
                    w = jnp.zeros((8, 128), f32)
                    for h in range(HI_V):
                        w = jnp.where(high == h, rows[8 * h : 8 * h + 8, cols], w)
                    w16 = jnp.concatenate([w, w], axis=0).astype(bf16)
                    row = spread_row(out_hi[r : r + 1, :], pat16)
                    for t in range(HI_V // 2):
                        v[4 * k + q, 16 * t : 16 * t + 16, cols] = jnp.where(
                            row == jnp.array(2 * t, bf16), w16, zero16
                        )
                    if forward:
                        mine = jnp.broadcast_to(out_hi[r : r + 1, :], (16, 128)) == z
                        v[4 * k + q, 8 * HI_V : 8 * HI_V + 16, cols] = jnp.where(
                            mine & (sub16 == 0), jnp.float32(1), jnp.float32(0)
                        ).astype(bf16)

        def scatter(j, v):
            total = None
            for k in range(N):
                out_lo = erx[slot(j, k), o_at : o_at + 8, :] & (LO - 1)
                for q in range(4):
                    part = lax.dot_general(hots(out_lo, q), v[4 * k + q, 0:width, :], NT, preferred_element_type=f32)
                    total = part if total is None else total + part
            acc[:, 0:width] += total

        def step(i):
            j = 2 * N * i
            scatter(jnp.maximum(j - N, 0), vb)
            for k in range(N):
                gather(j, va, k)
            scatter(j, va)
            for k in range(N):
                gather(j + N, vb, k)

        acc[...] = jnp.zeros_like(acc)
        vb[...] = jnp.zeros_like(vb)
        @pl.loop(0, M // (2 * N))
        def _(i):
            between(i)
            step(i)

        scatter(M - N, vb)
        return acc[:, 0:128].T

    def unpack(dst, total):
        for h in range(HI_V):
            both = fold8(total[8 * h : 8 * h + 8, :])
            dst[2 * h] = both[0:4, 0:128]
            dst[2 * h + 1] = both[0:4, 128:256]

    arrive("feat_wait", frx, M - 1, 2)
    with jax.named_scope("table"):
        table(frx)
    arrive("hub_wait", hubs, M - 1, 0)

    @pl.loop(1, G)
    def _(step):
        copy_to(hubs, hub_rows.at[g], 3, lax.rem(g + step, G), m).start()

    hub_rows[g] = hubs[...]
    with jax.named_scope("forward"):
        def edges_in_time(i):
            pl.when(i < 3)(lambda: hand_on(i + 1))
            others(i)

        total = aggregate(True, edges_in_time)
    with jax.named_scope("sums"):
        unpack(sums, total)
        over_members(sums, sumrx, 4)
        last = jnp.concatenate([acc[:, 128:144], jnp.zeros((LO, 112), f32)], axis=1).T
        degree = jnp.where(core == 0, last[0:1, 0:128], last[0:1, 128:256])
        inverse = 1.0 / jnp.maximum(degree, 1.0)
        for k in range(4, 8):
            fetches[k].wait()
        self_act = dot(feat[...], w_self[...]) + bias[...]
    with jax.named_scope("own_hubs"):
        own[...] = jnp.zeros_like(own)

        @pl.loop(0, M // 4)
        def _(i):
            total = None
            for k in range(4):
                src, dst = erx[4 * i + k, 0:8, :], erx[4 * i + k, 8:16, :]
                hub = src - LOCAL
                key = jnp.where(
                    (hub >= 0) & ((dst >> 7) == m), ((hub >> 8) << 7) + (dst & (ROWS - 1)), -1
                )
                for q in range(4):
                    part = lax.dot_general(hots(src & (LO - 1), q), hots(key, q), NT, preferred_element_type=f32)
                    total = part if total is None else total + part
            own[...] += total

        arrive("hubrow_wait", hub_rows, G - 1, 3)
        from_hubs = jnp.zeros((IN, ROWS), f32)
        for h in range(HI_H):
            rows = jnp.concatenate([hub_rows[8 * h + p, i] for p in range(8) for i in range(M)], axis=0)
            from_hubs = from_hubs + dot(rows.T, own[:, ROWS * h : ROWS * h + ROWS])
    arrive("sum_wait", sumrx, M - 1, 4)
    with jax.named_scope("dense"):
        mean_t = (joined(sumrx) + from_hubs) * inverse
        pre_act = self_act + dot(mean_t.T, w_neigh[...])
        sig = jax.nn.sigmoid(pre_act)
        pre_grad = cot[...] * sig * (1.0 + pre_act * (1.0 - sig))
        grad_s = dot(ft, pre_grad)
        grad_n = dot(mean_t, pre_grad)
        for p in range(G):
            half = grad_s if p < G // 2 else grad_n
            at = 16 * (p % (G // 2))
            g1s[p] = half[at : at + 16, :]
        over_groups(g1s, g1rx, 6)
        mean_grad_t = dot(w_neigh[...], pre_grad, NT) * inverse
        rows4(mgs, mean_grad_t)
        over_members(mgs, mgrx, 5)
    with jax.named_scope("hub_grads"):
        grad_b = jnp.sum(pre_grad, axis=0, keepdims=True)
        grad_b = jnp.concatenate([grad_b[:, 0:128], grad_b[:, 128:256], jnp.zeros((6, 128), f32)], axis=0)
        for h in range(HI_H):
            part = dot(own[:, ROWS * h : ROWS * h + ROWS], mean_grad_t, NT)
            for p in range(8):
                hgs[8 * h + p, 0:M, :] = part[M * p : M * p + M, :]
                hgs[8 * h + p, M : M + 8, :] = grad_b
        over_groups(hgs, hgrx, 7)
        hid[...] = pre_act * sig
        hid_out = pltpu.make_async_copy(hid, hid_o, osem.at[0])
        hid_out.start()
        fg[...] = dot(pre_grad, w_self[...], NT)

    scale = 1.0 / (float(G * M * ROWS) ** 0.5)

    def summed(src, n):
        total = src[0]
        for i in range(1, n):
            total = total + src[i]
        return total

    def reduce_groups():
        arrive("p1_wait", g1rx, G - 1, 6)
        total = summed(g1rx, G)
        for i in range(M):
            c = 128 * (i % 2)
            p2s[i] = total[i // 2 : i // 2 + 1, c : c + 128]
        over_members(p2s, p2rx, 8)

    def reduce_hubs():
        arrive("hubgrad_wait", hgrx, G - 1, 7)
        total = summed(hgrx, G)
        rest = total[M : M + 3, :]
        for i in range(M):
            h2s[i] = jnp.concatenate([total[i : i + 1, :], rest], axis=0)
        over_members(h2s, h2rx, 9)

    def reduce_members():
        arrive("p2_wait", p2rx, M - 1, 8)
        p3s[...] = summed(p2rx, M) * scale
        to_members(p3s, p3rx, 10)
        p3rx[m] = p3s[...]

    def collect_members():
        arrive("p3_wait", p3rx, M - 1, 10)
        for i in range(M):
            c = 128 * (i % 2)
            p4s[i // 2 : i // 2 + 1, c : c + 128] = p3rx[i]

        @pl.loop(1, G)
        def _(step):
            copy_to(p4s, p4rx.at[g], 11, lax.rem(g + step, G), m).start()

        p4rx[g] = p4s[...]

    reduce_groups()
    arrive("mean_wait", mgrx, M - 1, 5)
    with jax.named_scope("backward"):
        table(mgrx)
        def reductions(i):
            pl.when(i == 1)(reduce_hubs)
            pl.when(i == 3)(reduce_members)

        total = aggregate(False, reductions)
    with jax.named_scope("tail"):
        unpack(bs, total)
        over_members(bs, brx, 12)
        arrive("hubsum_wait", h2rx, M - 1, 9)
        total = summed(h2rx, M)
        gb[:, 0:128] = total[1:2, :] * scale
        gb[:, 128:256] = total[2:3, :] * scale
        first = lax.broadcasted_iota(i32, (8, 128), 0) == 0
        fg[0:8, :] += jnp.where(first, jnp.broadcast_to(total[0:1, :], (8, 128)), 0.0)
        collect_members()
        arrive("grad_wait", brx, M - 1, 12)
        fg[...] += joined(brx).T
        late = [
            pltpu.make_async_copy(fg, fg_o, osem.at[1]),
            pltpu.make_async_copy(gb, gb_o, osem.at[2]),
            pltpu.make_async_copy(p4rx.at[pl.ds(0, G // 2)], gs_o, osem.at[3]),
            pltpu.make_async_copy(p4rx.at[pl.ds(G // 2, G // 2)], gn_o, osem.at[4]),
        ]
        for copy in late[0:2]:
            copy.start()
        arrive("p4_wait", p4rx, G - 1, 11)
        for copy in late[2:4]:
            copy.start()

    for buf, n, k in (
        (hubs, M, 0), (erx, M, 1), (frx, M, 2), (hub_rows, G, 3), (sumrx, M, 4), (mgrx, M, 5), (g1rx, G, 6),
        (hgrx, G, 7), (p2rx, M, 8), (h2rx, M, 9), (p3rx, M, 10), (p4rx, G, 11), (brx, M, 12),
    ):
        wait(buf, n - 1, ssem.at[k])
    for copy in [hid_out] + late:
        copy.wait()


def write_out(*refs):
    for a, b in zip(refs[:5], refs[5:]):
        b[...] = a[...]


def on_device(features, w_self, w_neigh, bias, cotangent, edge_src, edge_dst, edge_count):
    anywhere, vmem = pl.BlockSpec(memory_space=pl.ANY), pl.BlockSpec(memory_space=pltpu.VMEM)
    quads = pltpu.VMEM((M, 4, 128), f32)
    lines = pltpu.VMEM((M, 1, 128), f32)
    args = [features, w_self, w_neigh, bias.reshape(1, HID), cotangent, edge_src, edge_dst, edge_count.reshape(1, 1)]
    scratch = [pltpu.VMEM(a.shape, a.dtype) for a in args] + [
        pltpu.VMEM((ROWS, HID), f32), pltpu.VMEM((ROWS, IN), f32), pltpu.VMEM((1, HID), f32),
        pltpu.VMEM((4 * N, 8 * HI_V + 16, 256), bf16), pltpu.VMEM((4 * N, 8 * HI_V + 16, 256), bf16),
        pltpu.VMEM((LO, 8 * HI_V + 16), f32), pltpu.VMEM((8 * HI_V, LO), bf16),
        pltpu.VMEM((LO, HI_H * ROWS), f32),
        lines, pltpu.VMEM((G, M, 1, 128), f32), pltpu.VMEM((M, 16, 128), i32),
        quads, quads, quads, quads, quads, quads,
        pltpu.VMEM((G, 16, HID), f32), pltpu.VMEM((G, 16, HID), f32), lines, lines,
        pltpu.VMEM((1, 128), f32), lines, pltpu.VMEM((16, HID), f32), pltpu.VMEM((G, 16, HID), f32),
        quads, quads, pltpu.VMEM((G, M + 8, 128), f32), pltpu.VMEM((G, M + 8, 128), f32), quads, quads,
        pltpu.SemaphoreType.DMA((13,)), pltpu.SemaphoreType.DMA((13,)), pltpu.SemaphoreType.DMA((M,)),
        pltpu.SemaphoreType.DMA((8,)), pltpu.SemaphoreType.DMA((5,)),
    ]
    shapes = [(ROWS, HID), (ROWS, IN), (G // 2, 16, HID), (G // 2, 16, HID), (1, HID)]
    results = pl.pallas_call(
        kernel,
        out_shape=[jax.ShapeDtypeStruct(s, f32) for s in shapes],
        in_specs=[anywhere] * 8,
        out_specs=[anywhere] * 5,
        scratch_shapes=scratch,
        compiler_params=pltpu.CompilerParams(
            collective_id=0, has_side_effects=True, vmem_limit_bytes=56 << 20
        ),
        name="sage",
    )(*args)
    final = [(ROWS, HID), (ROWS, IN), (IN, HID), (IN, HID), (1, HID)]
    results = pl.pallas_call(
        write_out,
        out_shape=[jax.ShapeDtypeStruct(s, f32) for s in final],
        in_specs=[vmem] * 5,
        out_specs=[vmem] * 5,
        name="write_out",
    )(*[r.reshape(s) for r, s in zip(results, final)])
    return (*results[:4], results[4].reshape(HID))


def solution(mesh):
    rows = P(("group", "member"), None)
    return jax.shard_map(
        on_device,
        mesh=mesh,
        in_specs=(rows, P(), P(), P(), rows, rows, rows, P(("group", "member"))),
        out_specs=(rows, rows, P(), P(), P()),
        check_vma=False,
    )
```

```python
import jax
import jax.numpy as jnp
from jax import lax
from jax.experimental import pallas as pl
from jax.experimental.pallas import tpu as pltpu
from jax.sharding import PartitionSpec as P

f32, bf16, i32 = jnp.float32, jnp.bfloat16, jnp.int32
MESH = pl.DeviceIdType.MESH
G, M = 16, 32
ROWS = 128
IN, HID = 128, 256
CHUNK = 1024
LOCAL = M * ROWS
LO = 256
HI_V = LOCAL // LO
HI_H = G * M // LO
N = 4
NT = (((1,), (1,)), ((), ()))


def halves(x):
    high = x.astype(bf16)
    return high, (x - high.astype(f32)).astype(bf16)


def dot(a, b, dims=(((1,), (0,)), ((), ()))):
    (a0, a1), (b0, b1) = halves(a), halves(b)

    def part(x, y):
        return lax.dot_general(x, y, dims, preferred_element_type=f32)

    return part(a0, b0) + (part(a0, b1) + part(a1, b0))


def split8(x):
    high = x.astype(bf16).astype(f32)
    return jnp.concatenate([high, x - high], axis=0)


def fold8(x):
    return x + pltpu.roll(x, 4, 0)


def each_far_first(me, n, send):
    send(lax.rem(me + n // 2, n))

    @pl.loop(1, n // 2)
    def _(near):
        send(lax.rem(me + n // 2 + near, n))
        send(lax.rem(me + n // 2 - near, n))


def kernel(
    feat_h, w_self_h, w_neigh_h, bias_h, cot_h, src_h, dst_h, cnt_h,
    hid, fg, gs, gn, gb,
    feat, w_self, w_neigh, bias, cot, e_src, e_dst, e_cnt,
    va, vb, acc, tab, own,
    hubs, hub_rows, erx, fts, frx, sums, sumrx, mgs, mgrx,
    g1s, g1rx, p2s, p2rx, p3s, p3rx, p4s, p4rx,
    bs, brx, hgs, hgrx, h2s, h2rx,
    ssem, rsem, esem, isem,
):
    g, m = lax.axis_index("group"), lax.axis_index("member")
    core, z = lax.rem(m, 2), m // 2
    sib = m + 1 - 2 * core
    sub16 = lax.broadcasted_iota(i32, (16, 128), 0)
    iota16 = sub16.astype(f32).astype(bf16)
    pat16 = (sub16 // 8).astype(f32).astype(bf16)
    one16 = jnp.ones((16, 128), bf16)
    zero16 = jnp.zeros((16, 128), bf16)

    barrier = pltpu.get_barrier_semaphore()
    with jax.named_scope("greet"):

        def greet(to):
            pl.semaphore_signal(barrier, inc=1, device_id=(g, to), device_id_type=MESH)

        each_far_first(m, M, greet)

        @pl.loop(1, G)
        def _(step):
            pl.semaphore_signal(barrier, inc=1, device_id=(lax.rem(g + step, G), m), device_id_type=MESH)

    fetches = [
        pltpu.make_async_copy(a, b, isem.at[k])
        for k, (a, b) in enumerate(
            [
                (feat_h, feat), (src_h, e_src), (dst_h, e_dst), (cnt_h, e_cnt),
                (w_self_h, w_self), (bias_h, bias), (w_neigh_h, w_neigh), (cot_h, cot),
            ]
        )
    ]
    for fetch in fetches:
        fetch.start()

    def copy_to(src, dst, k, gg, mm, recv=None):
        return pltpu.make_async_remote_copy(
            src_ref=src, dst_ref=dst, send_sem=ssem.at[k],
            recv_sem=rsem.at[k] if recv is None else recv,
            device_id=(gg, mm), device_id_type=MESH,
        )

    def over_members(src, dst, k):
        each_far_first(m, M, lambda to: copy_to(src.at[to], dst.at[m], k, g, to).start())
        dst[m] = src[m]

    def to_members(src, dst, k):
        each_far_first(m, M, lambda to: copy_to(src, dst.at[m], k, g, to).start())

    def over_groups(src, dst, k):
        @pl.loop(1, G)
        def _(step):
            to = lax.rem(g + step, G)
            copy_to(src.at[to], dst.at[g], k, to, m).start()
        dst[g] = src[g]

    def wait(buf, n, sem):
        view = buf.at[pl.ds(0, n)]
        pltpu.make_async_copy(view, view, sem).wait()

    def arrive(name, buf, n, k):
        with jax.named_scope(name):
            wait(buf, n, rsem.at[k])

    def rows4(dst, x):
        for i in range(M):
            dst[i] = x[4 * i : 4 * i + 4, :]

    def joined(src):
        return jnp.concatenate([src[i] for i in range(M)], axis=0)

    for k in range(4):
        fetches[k].wait()
    with jax.named_scope("pack"):
        ft = feat[...].T
        rows4(fts, ft)
        src = e_src[...]
        used = lax.broadcasted_iota(i32, (1, CHUNK), 1) < e_cnt[...]
        dst = jnp.where(used, e_dst[...], LOCAL)
        for r in range(8):
            erx[m, r : r + 1, :] = src[:, 128 * r : 128 * r + 128]
            erx[m, 8 + r : 9 + r, :] = dst[:, 128 * r : 128 * r + 128]

    with jax.named_scope("entry_wait"):
        pl.semaphore_wait(barrier, M - 1 + G - 1)

    over_members(fts, frx, 2)

    def edge_wait(slot):
        pltpu.make_async_copy(erx.at[slot], erx.at[slot], esem.at[slot]).wait()

    def edge_send(slot, to):
        copy_to(erx.at[slot], erx.at[slot], 1, g, to, esem.at[slot]).start()

    edge_send(m, sib)

    def nth_slot(n, other):
        odd = lax.rem(n, 2)
        ahead = odd * ((n + 1) // 2) + (1 - odd) * (M // 2 - n // 2)
        return lax.rem(z + ahead, M // 2) * 2 + (1 - core if other else core)

    @pl.loop(1, M // 2)
    def _(n):
        edge_send(m, nth_slot(n, False))

    hubs[m] = feat[0:1, :]
    to_members(hubs.at[m], hubs, 0)

    def hand_on(quarter):
        @pl.loop(0, 4)
        def _(k):
            slot = nth_slot(4 * quarter + k, False)
            edge_wait(slot)
            edge_send(slot, sib)

    def others(quarter):
        @pl.loop(0, 4)
        def _(k):
            edge_wait(nth_slot(4 * quarter + k, True))

    with jax.named_scope("edges_first"):
        @pl.loop(1, 8)
        def _(k):
            slot = nth_slot(k, False)
            edge_wait(slot)
            edge_send(slot, sib)

    def table(src):
        for t in range(HI_V // 2):
            for c in range(2):
                tab[16 * t : 16 * t + 16, 128 * c : 128 * c + 128] = jnp.concatenate(
                    [split8(src[4 * t + c]), split8(src[4 * t + 2 + c])], axis=0
                ).astype(bf16)

    def spread_row(row, pattern):
        return jnp.broadcast_to(row.astype(f32), (16, 128)).astype(bf16) - pattern

    def hots(low, q):
        halves = []
        for r in (2 * q, 2 * q + 1):
            row = spread_row(low[r : r + 1, :], iota16)
            halves.append(
                jnp.concatenate(
                    [jnp.where(row == jnp.array(16 * t, bf16), one16, zero16) for t in range(LO // 16)], axis=0
                )
            )
        return jnp.concatenate(halves, axis=1)

    def aggregate(forward, between):
        i_at, o_at = (0, 8) if forward else (8, 0)
        width = 8 * HI_V + (16 if forward else 0)

        def slot(c, k):
            return nth_slot(c // 2 + k // 2, k % 2 == 1)

        def gather(j, v, k):
            j = slot(j, k)
            ins, outs = erx[j, i_at : i_at + 8, :], erx[j, o_at : o_at + 8, :]
            in_lo, in_hi, out_hi = ins & (LO - 1), ins >> 8, outs >> 8
            for q in range(4):
                rows = jnp.dot(tab[...], hots(in_lo, q), preferred_element_type=f32)
                for c in range(2):
                    r = 2 * q + c
                    cols = slice(128 * c, 128 * c + 128)
                    high = jnp.broadcast_to(in_hi[r : r + 1, :], (8, 128))
                    w = jnp.zeros((8, 128), f32)
                    for h in range(HI_V):
                        w = jnp.where(high == h, rows[8 * h : 8 * h + 8, cols], w)
                    w16 = jnp.concatenate([w, w], axis=0).astype(bf16)
                    row = spread_row(out_hi[r : r + 1, :], pat16)
                    for t in range(HI_V // 2):
                        v[4 * k + q, 16 * t : 16 * t + 16, cols] = jnp.where(
                            row == jnp.array(2 * t, bf16), w16, zero16
                        )
                    if forward:
                        mine = jnp.broadcast_to(out_hi[r : r + 1, :], (16, 128)) == z
                        v[4 * k + q, 8 * HI_V : 8 * HI_V + 16, cols] = jnp.where(
                            mine & (sub16 == 0), jnp.float32(1), jnp.float32(0)
                        ).astype(bf16)

        def scatter(j, v):
            total = None
            for k in range(N):
                out_lo = erx[slot(j, k), o_at : o_at + 8, :] & (LO - 1)
                for q in range(4):
                    part = lax.dot_general(hots(out_lo, q), v[4 * k + q, 0:width, :], NT, preferred_element_type=f32)
                    total = part if total is None else total + part
            acc[:, 0:width] += total

        def step(i):
            j = 2 * N * i
            scatter(jnp.maximum(j - N, 0), vb)
            for k in range(N):
                gather(j, va, k)
            scatter(j, va)
            for k in range(N):
                gather(j + N, vb, k)

        acc[...] = jnp.zeros_like(acc)
        vb[...] = jnp.zeros_like(vb)
        @pl.loop(0, M // (2 * N))
        def _(i):
            between(i)
            step(i)

        scatter(M - N, vb)
        return acc[:, 0:128].T

    def unpack(dst, total):
        for h in range(HI_V):
            both = fold8(total[8 * h : 8 * h + 8, :])
            dst[2 * h] = both[0:4, 0:128]
            dst[2 * h + 1] = both[0:4, 128:256]

    arrive("feat_wait", frx, M - 1, 2)
    with jax.named_scope("table"):
        table(frx)
    with jax.named_scope("forward"):
        def share_hubs():
            arrive("hub_wait", hubs, M - 1, 0)

            @pl.loop(1, G)
            def _(step):
                copy_to(hubs, hub_rows.at[g], 3, lax.rem(g + step, G), m).start()

            hub_rows[g] = hubs[...]

        def edges_in_time(i):
            with jax.named_scope("near_edges"):
                pl.when((i == 1) | (i == 2))(lambda: hand_on(i + 1))
            with jax.named_scope("other_edges"):
                others(i)
            pl.when(i == 3)(share_hubs)

        total = aggregate(True, edges_in_time)
    with jax.named_scope("sums"):
        unpack(sums, total)
        over_members(sums, sumrx, 4)
        last = jnp.concatenate([acc[:, 128:144], jnp.zeros((LO, 112), f32)], axis=1).T
        degree = jnp.where(core == 0, last[0:1, 0:128], last[0:1, 128:256])
        inverse = 1.0 / jnp.maximum(degree, 1.0)
        for k in range(4, 8):
            fetches[k].wait()
        self_act = dot(feat[...], w_self[...]) + bias[...]
    with jax.named_scope("own_hubs"):
        own[...] = jnp.zeros_like(own)

        @pl.loop(0, M // 4)
        def _(i):
            total = None
            for k in range(4):
                src, dst = erx[4 * i + k, 0:8, :], erx[4 * i + k, 8:16, :]
                hub = src - LOCAL
                key = jnp.where(
                    (hub >= 0) & ((dst >> 7) == m), ((hub >> 8) << 7) + (dst & (ROWS - 1)), -1
                )
                for q in range(4):
                    part = lax.dot_general(hots(src & (LO - 1), q), hots(key, q), NT, preferred_element_type=f32)
                    total = part if total is None else total + part
            own[...] += total

        arrive("hubrow_wait", hub_rows, G - 1, 3)
        from_hubs = jnp.zeros((IN, ROWS), f32)
        for h in range(HI_H):
            rows = jnp.concatenate([hub_rows[8 * h + p, i] for p in range(8) for i in range(M)], axis=0)
            from_hubs = from_hubs + dot(rows.T, own[:, ROWS * h : ROWS * h + ROWS])
    arrive("sum_wait", sumrx, M - 1, 4)
    with jax.named_scope("dense"):
        mean_t = (joined(sumrx) + from_hubs) * inverse
        pre_act = self_act + dot(mean_t.T, w_neigh[...])
        sig = jax.nn.sigmoid(pre_act)
        pre_grad = cot[...] * sig * (1.0 + pre_act * (1.0 - sig))
        grad_s = dot(ft, pre_grad)
        grad_n = dot(mean_t, pre_grad)
        for p in range(G):
            half = grad_s if p < G // 2 else grad_n
            at = 16 * (p % (G // 2))
            g1s[p] = half[at : at + 16, :]
        over_groups(g1s, g1rx, 6)
        mean_grad_t = dot(w_neigh[...], pre_grad, NT) * inverse
        rows4(mgs, mean_grad_t)
        over_members(mgs, mgrx, 5)
    with jax.named_scope("hub_grads"):
        grad_b = jnp.sum(pre_grad, axis=0, keepdims=True)
        grad_b = jnp.concatenate([grad_b[:, 0:128], grad_b[:, 128:256], jnp.zeros((6, 128), f32)], axis=0)
        for h in range(HI_H):
            part = dot(own[:, ROWS * h : ROWS * h + ROWS], mean_grad_t, NT)
            for p in range(8):
                hgs[8 * h + p, 0:M, :] = part[M * p : M * p + M, :]
                hgs[8 * h + p, M : M + 8, :] = grad_b
        hid[...] = pre_act * sig
        fg[...] = dot(pre_grad, w_self[...], NT)

    scale = 1.0 / (float(G * M * ROWS) ** 0.5)

    def summed(src, n):
        total = src[0]
        for i in range(1, n):
            total = total + src[i]
        return total

    def reduce_groups():
        arrive("p1_wait", g1rx, G - 1, 6)
        total = summed(g1rx, G)
        for i in range(M):
            c = 128 * (i % 2)
            p2s[i] = total[i // 2 : i // 2 + 1, c : c + 128]
        over_members(p2s, p2rx, 8)

    def reduce_hubs():
        arrive("hubgrad_wait", hgrx, G - 1, 7)
        total = summed(hgrx, G)
        rest = total[M : M + 3, :]
        for i in range(M):
            h2s[i] = jnp.concatenate([total[i : i + 1, :], rest], axis=0)
        over_members(h2s, h2rx, 9)

    def reduce_members():
        arrive("p2_wait", p2rx, M - 1, 8)
        p3s[...] = summed(p2rx, M) * scale
        to_members(p3s, p3rx, 10)
        p3rx[m] = p3s[...]

    def collect_members():
        arrive("p3_wait", p3rx, M - 1, 10)
        for i in range(M):
            c = 128 * (i % 2)
            p4s[i // 2 : i // 2 + 1, c : c + 128] = p3rx[i]

        @pl.loop(1, G)
        def _(step):
            copy_to(p4s, p4rx.at[g], 11, lax.rem(g + step, G), m).start()

        p4rx[g] = p4s[...]

    reduce_groups()
    over_groups(hgs, hgrx, 7)
    arrive("mean_wait", mgrx, M - 1, 5)
    with jax.named_scope("backward"):
        table(mgrx)
        def reductions(i):
            pl.when(i == 2)(reduce_members)
            pl.when(i == 2)(reduce_hubs)

        total = aggregate(False, reductions)
    with jax.named_scope("tail"):
        unpack(bs, total)
        over_members(bs, brx, 12)
        collect_members()
        arrive("hubsum_wait", h2rx, M - 1, 9)
        total = summed(h2rx, M)
        gb[:, 0:128] = total[1:2, :] * scale
        gb[:, 128:256] = total[2:3, :] * scale
        first = lax.broadcasted_iota(i32, (8, 128), 0) == 0
        fg[0:8, :] += jnp.where(first, jnp.broadcast_to(total[0:1, :], (8, 128)), 0.0)
        arrive("grad_wait", brx, M - 1, 12)
        fg[...] += joined(brx).T
        arrive("p4_wait", p4rx, G - 1, 11)
        gs[...] = p4rx[0 : G // 2]
        gn[...] = p4rx[G // 2 : G]

    for buf, n, k in (
        (hubs, M, 0), (erx, M, 1), (frx, M, 2), (hub_rows, G, 3), (sumrx, M, 4), (mgrx, M, 5), (g1rx, G, 6),
        (hgrx, G, 7), (p2rx, M, 8), (h2rx, M, 9), (p3rx, M, 10), (p4rx, G, 11), (brx, M, 12),
    ):
        wait(buf, n - 1, ssem.at[k])


def write_out(*refs):
    for a, b in zip(refs[:5], refs[5:]):
        b[...] = a[...]


def on_device(features, w_self, w_neigh, bias, cotangent, edge_src, edge_dst, edge_count):
    anywhere, vmem = pl.BlockSpec(memory_space=pl.ANY), pl.BlockSpec(memory_space=pltpu.VMEM)
    quads = pltpu.VMEM((M, 4, 128), f32)
    lines = pltpu.VMEM((M, 1, 128), f32)
    args = [features, w_self, w_neigh, bias.reshape(1, HID), cotangent, edge_src, edge_dst, edge_count.reshape(1, 1)]
    scratch = [pltpu.VMEM(a.shape, a.dtype) for a in args] + [
        pltpu.VMEM((4 * N, 8 * HI_V + 16, 256), bf16), pltpu.VMEM((4 * N, 8 * HI_V + 16, 256), bf16),
        pltpu.VMEM((LO, 8 * HI_V + 16), f32), pltpu.VMEM((8 * HI_V, LO), bf16),
        pltpu.VMEM((LO, HI_H * ROWS), f32),
        lines, pltpu.VMEM((G, M, 1, 128), f32), pltpu.VMEM((M, 16, 128), i32),
        quads, quads, quads, quads, quads, quads,
        pltpu.VMEM((G, 16, HID), f32), pltpu.VMEM((G, 16, HID), f32), lines, lines,
        pltpu.VMEM((1, 128), f32), lines, pltpu.VMEM((16, HID), f32), pltpu.VMEM((G, 16, HID), f32),
        quads, quads, pltpu.VMEM((G, M + 8, 128), f32), pltpu.VMEM((G, M + 8, 128), f32), quads, quads,
        pltpu.SemaphoreType.DMA((13,)), pltpu.SemaphoreType.DMA((13,)), pltpu.SemaphoreType.DMA((M,)),
        pltpu.SemaphoreType.DMA((8,)),
    ]
    shapes = [(ROWS, HID), (ROWS, IN), (G // 2, 16, HID), (G // 2, 16, HID), (1, HID)]
    results = pl.pallas_call(
        kernel,
        out_shape=[pltpu.VMEM(s, f32) for s in shapes],
        in_specs=[anywhere] * 8,
        out_specs=[vmem] * 5,
        scratch_shapes=scratch,
        compiler_params=pltpu.CompilerParams(
            collective_id=0, has_side_effects=True, vmem_limit_bytes=56 << 20
        ),
        name="sage",
    )(*args)
    final = [(ROWS, HID), (ROWS, IN), (IN, HID), (IN, HID), (1, HID)]
    results = pl.pallas_call(
        write_out,
        out_shape=[jax.ShapeDtypeStruct(s, f32) for s in final],
        in_specs=[vmem] * 5,
        out_specs=[vmem] * 5,
        compiler_params=pltpu.CompilerParams(vmem_limit_bytes=4 << 20),
        name="write_out",
    )(*[r.reshape(s) for r, s in zip(results, final)])
    return (*results[:4], results[4].reshape(HID))


def solution(mesh):
    rows = P(("group", "member"), None)
    return jax.shard_map(
        on_device,
        mesh=mesh,
        in_specs=(rows, P(), P(), P(), rows, rows, rows, P(("group", "member"))),
        out_specs=(rows, rows, P(), P(), P()),
        check_vma=False,
    )
```

```python
import jax
import jax.numpy as jnp
from jax import lax
from jax.experimental import pallas as pl
from jax.experimental.pallas import tpu as pltpu
from jax.sharding import PartitionSpec as P

f32, bf16, i32 = jnp.float32, jnp.bfloat16, jnp.int32
MESH = pl.DeviceIdType.MESH
G, M = 16, 32
ROWS = 128
IN, HID = 128, 256
CHUNK = 1024
LOCAL = M * ROWS
LO = 256
HI_V = LOCAL // LO
HI_H = G * M // LO
N = 4
NT = (((1,), (1,)), ((), ()))


def halves(x):
    high = x.astype(bf16)
    return high, (x - high.astype(f32)).astype(bf16)


def dot(a, b, dims=(((1,), (0,)), ((), ()))):
    (a0, a1), (b0, b1) = halves(a), halves(b)

    def part(x, y):
        return lax.dot_general(x, y, dims, preferred_element_type=f32)

    return part(a0, b0) + (part(a0, b1) + part(a1, b0))


def split8(x):
    high = x.astype(bf16).astype(f32)
    return jnp.concatenate([high, x - high], axis=0)


def fold8(x):
    return x + pltpu.roll(x, 4, 0)


def each_far_first(me, n, send):
    send(lax.rem(me + n // 2, n))

    @pl.loop(1, n // 2)
    def _(near):
        send(lax.rem(me + n // 2 + near, n))
        send(lax.rem(me + n // 2 - near, n))


def kernel(
    feat_h, w_self_h, w_neigh_h, bias_h, cot_h, src_h, dst_h, cnt_h,
    hid, fg, gs, gn, gb,
    feat, w_self, w_neigh, bias, cot, e_src, e_dst, e_cnt,
    va, vb, acc, tab, own,
    hubs, hub_rows, erx, fts, frx, sums, sumrx, mgs, mgrx,
    g1s, g1rx, p2s, p2rx, p3s, p3rx, p4s, p4rx,
    bs, brx, hgs, hgrx, h2s, h2rx,
    ssem, rsem, esem, isem,
):
    g, m = lax.axis_index("group"), lax.axis_index("member")
    core, z = lax.rem(m, 2), m // 2
    sib = m + 1 - 2 * core
    sub16 = lax.broadcasted_iota(i32, (16, 128), 0)
    iota16 = sub16.astype(f32).astype(bf16)
    pat16 = (sub16 // 8).astype(f32).astype(bf16)
    one16 = jnp.ones((16, 128), bf16)
    zero16 = jnp.zeros((16, 128), bf16)

    barrier = pltpu.get_barrier_semaphore()
    with jax.named_scope("greet"):

        def greet(to):
            pl.semaphore_signal(barrier, inc=1, device_id=(g, to), device_id_type=MESH)

        each_far_first(m, M, greet)

        @pl.loop(1, G)
        def _(step):
            pl.semaphore_signal(barrier, inc=1, device_id=(lax.rem(g + step, G), m), device_id_type=MESH)

    fetches = [
        pltpu.make_async_copy(a, b, isem.at[k])
        for k, (a, b) in enumerate(
            [
                (feat_h, feat), (src_h, e_src), (dst_h, e_dst), (cnt_h, e_cnt),
                (w_self_h, w_self), (bias_h, bias), (w_neigh_h, w_neigh), (cot_h, cot),
            ]
        )
    ]
    for fetch in fetches:
        fetch.start()

    def copy_to(src, dst, k, gg, mm, recv=None):
        return pltpu.make_async_remote_copy(
            src_ref=src, dst_ref=dst, send_sem=ssem.at[k],
            recv_sem=rsem.at[k] if recv is None else recv,
            device_id=(gg, mm), device_id_type=MESH,
        )

    def over_members(src, dst, k):
        each_far_first(m, M, lambda to: copy_to(src.at[to], dst.at[m], k, g, to).start())
        dst[m] = src[m]

    def to_members(src, dst, k):
        each_far_first(m, M, lambda to: copy_to(src, dst.at[m], k, g, to).start())

    def over_groups(src, dst, k):
        @pl.loop(1, G)
        def _(step):
            to = lax.rem(g + step, G)
            copy_to(src.at[to], dst.at[g], k, to, m).start()
        dst[g] = src[g]

    def wait(buf, n, sem):
        view = buf.at[pl.ds(0, n)]
        pltpu.make_async_copy(view, view, sem).wait()

    def arrive(name, buf, n, k):
        with jax.named_scope(name):
            wait(buf, n, rsem.at[k])

    def rows4(dst, x):
        for i in range(M):
            dst[i] = x[4 * i : 4 * i + 4, :]

    def joined(src):
        return jnp.concatenate([src[i] for i in range(M)], axis=0)

    for k in range(4):
        fetches[k].wait()
    with jax.named_scope("pack"):
        ft = feat[...].T
        rows4(fts, ft)
        src = e_src[...]
        used = lax.broadcasted_iota(i32, (1, CHUNK), 1) < e_cnt[...]
        dst = jnp.where(used, e_dst[...], LOCAL)
        for r in range(8):
            erx[m, r : r + 1, :] = src[:, 128 * r : 128 * r + 128]
            erx[m, 8 + r : 9 + r, :] = dst[:, 128 * r : 128 * r + 128]

    with jax.named_scope("entry_wait"):
        pl.semaphore_wait(barrier, M - 1 + G - 1)

    over_members(fts, frx, 2)

    def edge_wait(slot):
        pltpu.make_async_copy(erx.at[slot], erx.at[slot], esem.at[slot]).wait()

    def edge_send(slot, to):
        copy_to(erx.at[slot], erx.at[slot], 1, g, to, esem.at[slot]).start()

    edge_send(m, sib)

    def nth_slot(n, other):
        odd = lax.rem(n, 2)
        ahead = odd * ((n + 1) // 2) + (1 - odd) * (M // 2 - n // 2)
        return lax.rem(z + ahead, M // 2) * 2 + (1 - core if other else core)

    @pl.loop(1, M // 2)
    def _(n):
        edge_send(m, nth_slot(n, False))

    hubs[m] = feat[0:1, :]
    to_members(hubs.at[m], hubs, 0)

    def hand_on(quarter):
        @pl.loop(0, 4)
        def _(k):
            slot = nth_slot(4 * quarter + k, False)
            edge_wait(slot)
            edge_send(slot, sib)

    def others(quarter):
        @pl.loop(0, 4)
        def _(k):
            edge_wait(nth_slot(4 * quarter + k, True))

    with jax.named_scope("edges_first"):
        @pl.loop(1, 8)
        def _(k):
            slot = nth_slot(k, False)
            edge_wait(slot)
            edge_send(slot, sib)

    def table(src):
        for t in range(HI_V // 2):
            for c in range(2):
                tab[16 * t : 16 * t + 16, 128 * c : 128 * c + 128] = jnp.concatenate(
                    [split8(src[4 * t + c]), split8(src[4 * t + 2 + c])], axis=0
                ).astype(bf16)

    def spread_row(row, pattern):
        return jnp.broadcast_to(row.astype(f32), (16, 128)).astype(bf16) - pattern

    def hots(low, q):
        halves = []
        for r in (2 * q, 2 * q + 1):
            row = spread_row(low[r : r + 1, :], iota16)
            halves.append(
                jnp.concatenate(
                    [jnp.where(row == jnp.array(16 * t, bf16), one16, zero16) for t in range(LO // 16)], axis=0
                )
            )
        return jnp.concatenate(halves, axis=1)

    def aggregate(forward, between):
        i_at, o_at = (0, 8) if forward else (8, 0)
        width = 8 * HI_V + (16 if forward else 0)

        def slot(c, k):
            return nth_slot(c // 2 + k // 2, k % 2 == 1)

        def gather(j, v, k):
            j = slot(j, k)
            ins, outs = erx[j, i_at : i_at + 8, :], erx[j, o_at : o_at + 8, :]
            in_lo, in_hi, out_hi = ins & (LO - 1), ins >> 8, outs >> 8
            for q in range(4):
                rows = jnp.dot(tab[...], hots(in_lo, q), preferred_element_type=f32)
                for c in range(2):
                    r = 2 * q + c
                    cols = slice(128 * c, 128 * c + 128)
                    high = jnp.broadcast_to(in_hi[r : r + 1, :], (8, 128))
                    w = jnp.zeros((8, 128), f32)
                    for h in range(HI_V):
                        w = jnp.where(high == h, rows[8 * h : 8 * h + 8, cols], w)
                    w16 = jnp.concatenate([w, w], axis=0).astype(bf16)
                    row = spread_row(out_hi[r : r + 1, :], pat16)
                    for t in range(HI_V // 2):
                        v[4 * k + q, 16 * t : 16 * t + 16, cols] = jnp.where(
                            row == jnp.array(2 * t, bf16), w16, zero16
                        )
                    if forward:
                        mine = jnp.broadcast_to(out_hi[r : r + 1, :], (16, 128)) == z
                        v[4 * k + q, 8 * HI_V : 8 * HI_V + 16, cols] = jnp.where(
                            mine & (sub16 == 0), jnp.float32(1), jnp.float32(0)
                        ).astype(bf16)

        def scatter(j, v):
            total = None
            for k in range(N):
                out_lo = erx[slot(j, k), o_at : o_at + 8, :] & (LO - 1)
                for q in range(4):
                    part = lax.dot_general(hots(out_lo, q), v[4 * k + q, 0:width, :], NT, preferred_element_type=f32)
                    total = part if total is None else total + part
            acc[:, 0:width] += total

        def step(i):
            j = 2 * N * i
            scatter(jnp.maximum(j - N, 0), vb)
            for k in range(N):
                gather(j, va, k)
            scatter(j, va)
            for k in range(N):
                gather(j + N, vb, k)

        acc[...] = jnp.zeros_like(acc)
        vb[...] = jnp.zeros_like(vb)
        @pl.loop(0, M // (2 * N))
        def _(i):
            between(i)
            step(i)

        scatter(M - N, vb)
        return acc[:, 0:128].T

    def unpack(dst, total):
        for h in range(HI_V):
            both = fold8(total[8 * h : 8 * h + 8, :])
            dst[2 * h] = both[0:4, 0:128]
            dst[2 * h + 1] = both[0:4, 128:256]

    arrive("feat_wait", frx, M - 1, 2)
    with jax.named_scope("table"):
        table(frx)
    with jax.named_scope("forward"):
        def share_hubs():
            arrive("hub_wait", hubs, M - 1, 0)

            @pl.loop(1, G)
            def _(step):
                copy_to(hubs, hub_rows.at[g], 3, lax.rem(g + step, G), m).start()

            hub_rows[g] = hubs[...]

        def edges_in_time(i):
            with jax.named_scope("near_edges"):
                pl.when((i == 1) | (i == 2))(lambda: hand_on(i + 1))
            with jax.named_scope("other_edges"):
                others(i)
            pl.when(i == 3)(share_hubs)

        total = aggregate(True, edges_in_time)
    with jax.named_scope("sums"):
        unpack(sums, total)
        over_members(sums, sumrx, 4)
        last = jnp.concatenate([acc[:, 128:144], jnp.zeros((LO, 112), f32)], axis=1).T
        degree = jnp.where(core == 0, last[0:1, 0:128], last[0:1, 128:256])
        inverse = 1.0 / jnp.maximum(degree, 1.0)
        for k in range(4, 8):
            fetches[k].wait()
        self_act = dot(feat[...], w_self[...]) + bias[...]
    with jax.named_scope("own_hubs"):
        own[...] = jnp.zeros_like(own)

        @pl.loop(0, M // 4)
        def _(i):
            total = None
            for k in range(4):
                src, dst = erx[4 * i + k, 0:8, :], erx[4 * i + k, 8:16, :]
                hub = src - LOCAL
                key = jnp.where(
                    (hub >= 0) & ((dst >> 7) == m), ((hub >> 8) << 7) + (dst & (ROWS - 1)), -1
                )
                for q in range(4):
                    part = lax.dot_general(hots(src & (LO - 1), q), hots(key, q), NT, preferred_element_type=f32)
                    total = part if total is None else total + part
            own[...] += total

        arrive("hubrow_wait", hub_rows, G - 1, 3)
        from_hubs = jnp.zeros((IN, ROWS), f32)
        for h in range(HI_H):
            rows = jnp.concatenate([hub_rows[8 * h + p, i] for p in range(8) for i in range(M)], axis=0)
            from_hubs = from_hubs + dot(rows.T, own[:, ROWS * h : ROWS * h + ROWS])
    arrive("sum_wait", sumrx, M - 1, 4)
    with jax.named_scope("dense"):
        mean_t = (joined(sumrx) + from_hubs) * inverse
        pre_act = self_act + dot(mean_t.T, w_neigh[...])
        sig = jax.nn.sigmoid(pre_act)
        pre_grad = cot[...] * sig * (1.0 + pre_act * (1.0 - sig))
        grad_s = dot(ft, pre_grad)
        grad_n = dot(mean_t, pre_grad)
        for p in range(G):
            half = grad_s if p < G // 2 else grad_n
            at = 16 * (p % (G // 2))
            g1s[p] = half[at : at + 16, :]
        over_groups(g1s, g1rx, 6)
        mean_grad_t = dot(w_neigh[...], pre_grad, NT) * inverse
        rows4(mgs, mean_grad_t)
        over_members(mgs, mgrx, 5)
    with jax.named_scope("hub_grads"):
        grad_b = jnp.sum(pre_grad, axis=0, keepdims=True)
        grad_b = jnp.concatenate([grad_b[:, 0:128], grad_b[:, 128:256], jnp.zeros((6, 128), f32)], axis=0)
        for h in range(HI_H):
            part = dot(own[:, ROWS * h : ROWS * h + ROWS], mean_grad_t, NT)
            for p in range(8):
                hgs[8 * h + p, 0:M, :] = part[M * p : M * p + M, :]
                hgs[8 * h + p, M : M + 8, :] = grad_b
        hid[...] = pre_act * sig
        fg[...] = dot(pre_grad, w_self[...], NT)

    scale = 1.0 / (float(G * M * ROWS) ** 0.5)

    def summed(src, n):
        total = src[0]
        for i in range(1, n):
            total = total + src[i]
        return total

    def reduce_groups():
        arrive("p1_wait", g1rx, G - 1, 6)
        total = summed(g1rx, G)
        for i in range(M):
            c = 128 * (i % 2)
            p2s[i] = total[i // 2 : i // 2 + 1, c : c + 128]
        over_members(p2s, p2rx, 8)

    def reduce_hubs():
        arrive("hubgrad_wait", hgrx, G - 1, 7)
        total = summed(hgrx, G)
        rest = total[M : M + 3, :]
        for i in range(M):
            h2s[i] = jnp.concatenate([total[i : i + 1, :], rest], axis=0)
        over_members(h2s, h2rx, 9)

    def reduce_members():
        arrive("p2_wait", p2rx, M - 1, 8)
        p3s[...] = summed(p2rx, M) * scale
        to_members(p3s, p3rx, 10)
        p3rx[m] = p3s[...]

    def collect_members():
        arrive("p3_wait", p3rx, M - 1, 10)
        for i in range(M):
            c = 128 * (i % 2)
            p4s[i // 2 : i // 2 + 1, c : c + 128] = p3rx[i]

        @pl.loop(1, G)
        def _(step):
            copy_to(p4s, p4rx.at[g], 11, lax.rem(g + step, G), m).start()

        p4rx[g] = p4s[...]

    reduce_groups()
    over_groups(hgs, hgrx, 7)
    arrive("mean_wait", mgrx, M - 1, 5)
    with jax.named_scope("backward"):
        table(mgrx)
        def reductions(i):
            pl.when(i == 2)(reduce_members)
            pl.when(i == 2)(reduce_hubs)

        total = aggregate(False, reductions)
    with jax.named_scope("tail"):
        unpack(bs, total)
        over_members(bs, brx, 12)
        collect_members()
        arrive("hubsum_wait", h2rx, M - 1, 9)
        total = summed(h2rx, M)
        gb[:, 0:128] = total[1:2, :] * scale
        gb[:, 128:256] = total[2:3, :] * scale
        first = lax.broadcasted_iota(i32, (8, 128), 0) == 0
        fg[0:8, :] += jnp.where(first, jnp.broadcast_to(total[0:1, :], (8, 128)), 0.0)
        for buf, n, k in (
            (hubs, M, 0), (erx, M, 1), (frx, M, 2), (hub_rows, G, 3), (sumrx, M, 4), (mgrx, M, 5), (g1rx, G, 6),
            (hgrx, G, 7), (p2rx, M, 8), (h2rx, M, 9), (p3rx, M, 10), (p4rx, G, 11), (brx, M, 12),
        ):
            wait(buf, n - 1, ssem.at[k])
        arrive("grad_wait", brx, M - 1, 12)
        fg[...] += joined(brx).T
        arrive("p4_wait", p4rx, G - 1, 11)
        gs[...] = p4rx[0 : G // 2]
        gn[...] = p4rx[G // 2 : G]


def write_out(*refs):
    for a, b in zip(refs[:5], refs[5:]):
        b[...] = a[...]


def on_device(features, w_self, w_neigh, bias, cotangent, edge_src, edge_dst, edge_count):
    anywhere, vmem = pl.BlockSpec(memory_space=pl.ANY), pl.BlockSpec(memory_space=pltpu.VMEM)
    quads = pltpu.VMEM((M, 4, 128), f32)
    lines = pltpu.VMEM((M, 1, 128), f32)
    args = [features, w_self, w_neigh, bias.reshape(1, HID), cotangent, edge_src, edge_dst, edge_count.reshape(1, 1)]
    scratch = [pltpu.VMEM(a.shape, a.dtype) for a in args] + [
        pltpu.VMEM((4 * N, 8 * HI_V + 16, 256), bf16), pltpu.VMEM((4 * N, 8 * HI_V + 16, 256), bf16),
        pltpu.VMEM((LO, 8 * HI_V + 16), f32), pltpu.VMEM((8 * HI_V, LO), bf16),
        pltpu.VMEM((LO, HI_H * ROWS), f32),
        lines, pltpu.VMEM((G, M, 1, 128), f32), pltpu.VMEM((M, 16, 128), i32),
        quads, quads, quads, quads, quads, quads,
        pltpu.VMEM((G, 16, HID), f32), pltpu.VMEM((G, 16, HID), f32), lines, lines,
        pltpu.VMEM((1, 128), f32), lines, pltpu.VMEM((16, HID), f32), pltpu.VMEM((G, 16, HID), f32),
        quads, quads, pltpu.VMEM((G, M + 8, 128), f32), pltpu.VMEM((G, M + 8, 128), f32), quads, quads,
        pltpu.SemaphoreType.DMA((13,)), pltpu.SemaphoreType.DMA((13,)), pltpu.SemaphoreType.DMA((M,)),
        pltpu.SemaphoreType.DMA((8,)),
    ]
    shapes = [(ROWS, HID), (ROWS, IN), (G // 2, 16, HID), (G // 2, 16, HID), (1, HID)]
    results = pl.pallas_call(
        kernel,
        out_shape=[pltpu.VMEM(s, f32) for s in shapes],
        in_specs=[anywhere] * 8,
        out_specs=[vmem] * 5,
        scratch_shapes=scratch,
        compiler_params=pltpu.CompilerParams(
            collective_id=0, has_side_effects=True, vmem_limit_bytes=56 << 20
        ),
        name="sage",
    )(*args)
    final = [(ROWS, HID), (ROWS, IN), (IN, HID), (IN, HID), (1, HID)]
    results = pl.pallas_call(
        write_out,
        out_shape=[jax.ShapeDtypeStruct(s, f32) for s in final],
        in_specs=[vmem] * 5,
        out_specs=[vmem] * 5,
        compiler_params=pltpu.CompilerParams(vmem_limit_bytes=4 << 20),
        name="write_out",
    )(*[r.reshape(s) for r, s in zip(results, final)])
    return (*results[:4], results[4].reshape(HID))


def solution(mesh):
    rows = P(("group", "member"), None)
    return jax.shard_map(
        on_device,
        mesh=mesh,
        in_specs=(rows, P(), P(), P(), rows, rows, rows, P(("group", "member"))),
        out_specs=(rows, rows, P(), P(), P()),
        check_vma=False,
    )
```
